256 devices in a mesh: image: 16 (over z_lo, x, core), space: 16 (over z_hi, y).
Axes of the slice: x: 4, y: 4, z: 8 (z_hi: 4, z_lo: 2; z = z_hi * 2 + z_lo), core: 2. Of those that a mesh axis runs over, the one named last changes fastest.
Arguments:
- magnetization: float32 [16, 3, 128, 128, 128], P('image', None, 'space'), may hold values from -1 to 1, as said below
- region_labels: int32 [128, 128, 128], P('space'), may hold values from 0 to 7
- demag_kernel: float32 [6, 128, 128, 128], P(None, None, 'space'), may hold values from -0.3 to 0.6, as said below
- anisotropy: float32 [8], replicated, may hold values from 0.2 to 2
- stiffness: float32 [8], replicated, may hold values from 0.05 to 0.5
Outputs:
- relaxed_path: float32 [16, 3, 128, 128, 128], P('image', None, 'space')
- band_force: float32 [16, 3, 128, 128, 128], P('image', None, 'space')
The draws below stay inside these ranges and needn't reach their ends.
Inputs may be any that keep to these rules, and one draw needn't show every extreme that they name: `magnetization`: each cell's three components form a unit vector; the first and last images are the band's fixed ends. The tensor is even in the wave number: demag_kernel[c, i, j, k] equals demag_kernel[c, (G - i) % G, (G - j) % G, (G - k) % G] with G = 128.
All inputs are finite; a program needn't handle non-finite values.
Results may differ from the reference program's by a relative error of at most 0.0003.
Values sent between devices are 32-bit elements; how exact they have to be, the bound alone decides.
A program may use at most 128 MiB of HBM per device.

```python
import math
import jax
import jax.numpy as jnp
from jax import lax

G = 128
REGIONS = 8
ITERS = 1
IMAGES = 16


def draw_magnetization(key, part):
    key = jax.random.fold_in(key, 7)
    key_azimuth, key_noise = jax.random.split(key, 2)
    image_pos = jnp.arange(IMAGES, dtype=jnp.float32)[:, None, None, None] / (IMAGES - 1)
    depth_frac = jnp.arange(G, dtype=jnp.float32)[None, :, None, None] / (G - 1)
    polar_angle = math.pi * image_pos ** 1.5 * (1.0 / 3.0 + 2.0 / 3.0 * depth_frac)
    azimuth = jax.random.uniform(key_azimuth, (1, G, G, G), jnp.float32, -math.pi, math.pi)
    amplitude = 0.15
    base_dir = jnp.stack([jnp.sin(polar_angle) * jnp.cos(azimuth), jnp.sin(polar_angle) * jnp.sin(azimuth), jnp.cos(polar_angle) + 0.0 * azimuth], axis=1)
    noise_part = jax.random.uniform(key_noise, (IMAGES, 3, G, G, G), jnp.float32, -1.0, 1.0) * amplitude
    vector = base_dir + noise_part
    return vector / jnp.sqrt(jnp.sum(vector * vector, axis=1, keepdims=True))


def draw_demag_kernel(key, part):
    key = jax.random.fold_in(key, 11)
    raw_values = jax.random.uniform(key, (6, G, G, G), jnp.float32, -0.3, 0.6)
    mirrored = raw_values
    for axis_dim in (1, 2, 3):
        mirrored = jnp.roll(jnp.flip(mirrored, axis_dim), 1, axis_dim)
    return 0.5 * (raw_values + mirrored)


def plant(drawn, stream_key, least, high):
    extent = drawn.shape
    place = [jax.random.randint(jax.random.fold_in(stream_key, axis), (), 0, extent[axis]) for axis in range(len(extent))]
    drawn = drawn.at[tuple(place)].set(least)
    longest = extent.index(max(extent))
    place[longest] = (place[longest] + 1) % extent[longest]
    return drawn.at[tuple(place)].set(high)


def setup_inputs(seed: int = 0) -> dict:
    splits = jax.random.split(jax.random.key(seed), 6)
    return {
        "magnetization": draw_magnetization(jax.random.fold_in(splits[5], 71), 0),
        "region_labels": plant(jax.random.randint(splits[1], (G, G, G), 0, REGIONS), jax.random.fold_in(splits[1], 1), 0, REGIONS - 1).astype(jnp.int32),
        "demag_kernel": draw_demag_kernel(jax.random.fold_in(splits[5], 71), 0),
        "anisotropy": jnp.clip(jnp.exp(jax.random.uniform(splits[3], (REGIONS,), jnp.float32, math.log(0.2), math.log(2.0))), 0.2, 2.0),
        "stiffness": jnp.clip(jnp.exp(jax.random.uniform(splits[4], (REGIONS,), jnp.float32, math.log(0.05), math.log(0.5))), 0.05, 0.5),
    }


STEP_SIZE = 0.2
SPRING = 4.0
EPSILON = 1e-06
TENSOR_ROWS = ((0, 3, 4), (3, 1, 5), (4, 5, 2))

def region_value(region_labels, region_table):
    total = jnp.zeros(region_labels.shape, jnp.float32)
    for region in range(REGIONS):
        total = total + jnp.where(region_labels == region, region_table[region], jnp.zeros((), jnp.float32))
    return total

def demag_field(moment, demag_kernel):
    spectrum = jnp.fft.fftn(moment, axes=(1, 2, 3))
    pieces = []
    for kernel_row in TENSOR_ROWS:
        pieces.append(demag_kernel[kernel_row[0]] * spectrum[0] + demag_kernel[kernel_row[1]] * spectrum[1] + demag_kernel[kernel_row[2]] * spectrum[2])
    return -jnp.real(jnp.fft.ifftn(jnp.stack(pieces), axes=(1, 2, 3)))

def angle_sum(leading, trailing):
    cross_x = leading[1] * trailing[2] - leading[2] * trailing[1]
    cross_y = leading[2] * trailing[0] - leading[0] * trailing[2]
    cross_z = leading[0] * trailing[1] - leading[1] * trailing[0]
    sine_term = jnp.sqrt(cross_x * cross_x + cross_y * cross_y + cross_z * cross_z)
    cosine = lax.optimization_barrier(jnp.sum(leading * trailing, axis=0))
    return jnp.sum(jnp.arctan2(sine_term, cosine) ** 2)

def effective_field(moment, demag_kernel, anis_cell, stiff_cell):
    laplace = -6.0 * moment
    for axis_dim in (1, 2, 3):
        laplace = laplace + jnp.roll(moment, 1, axis_dim) + jnp.roll(moment, -1, axis_dim)
    field_sum = stiff_cell * laplace + demag_field(moment, demag_kernel)
    return field_sum.at[2].add(2.0 * anis_cell * moment[2])

def image_force(image_index, band, demag_kernel, anis_cell, stiff_cell):
    count = band.shape[0]
    cell_count = band.shape[2] * band.shape[3] * band.shape[4]
    moment = lax.dynamic_index_in_dim(band, image_index, 0, keepdims=False)
    preceding = lax.dynamic_index_in_dim(band, jnp.maximum(image_index - 1, 0), 0, keepdims=False) * (image_index > 0).astype(jnp.float32)
    following = lax.dynamic_index_in_dim(band, jnp.minimum(image_index + 1, count - 1), 0, keepdims=False) * (image_index < count - 1).astype(jnp.float32)
    gradient = -effective_field(moment, demag_kernel, anis_cell, stiff_cell)
    g_perp = gradient - lax.optimization_barrier(jnp.sum(gradient * moment, axis=0)) * moment
    tangent = following - preceding
    tangent = tangent - lax.optimization_barrier(jnp.sum(tangent * moment, axis=0)) * moment
    tangent_sq = jnp.sum(tangent * tangent)
    slope_sum = jnp.sum(g_perp * tangent)
    next_sq = angle_sum(moment, following)
    prev_sq = angle_sum(preceding, moment)
    factor = jnp.sqrt(cell_count / (tangent_sq + EPSILON))
    unit_tangent = tangent * factor
    along_term = slope_sum * factor / cell_count
    spring_term = SPRING * (jnp.sqrt(next_sq / cell_count) - jnp.sqrt(prev_sq / cell_count))
    movable = ((image_index > 0) & (image_index < count - 1)).astype(jnp.float32)
    return movable * (-g_perp + (along_term + spring_term) * unit_tangent)

def reference(magnetization, region_labels, demag_kernel, anisotropy, stiffness):
    anis_cell = region_value(region_labels, anisotropy)
    stiff_cell = region_value(region_labels, stiffness)
    band = magnetization
    band_force = jnp.zeros_like(band)
    for sweep_index in range(ITERS):
        current = band
        band_force = lax.map(lambda image_index: image_force(image_index, current, demag_kernel, anis_cell, stiff_cell), jnp.arange(band.shape[0], dtype=jnp.int32))
        stepped = current + STEP_SIZE * band_force
        band = stepped / jnp.sqrt(lax.optimization_barrier(jnp.sum(stepped * stepped, axis=1, keepdims=True)))
    return (band, band_force)
```

```python
import functools
import math

import jax
import jax.numpy as jnp
import numpy as np
from jax import lax
from jax.experimental import pallas as pl
from jax.experimental.pallas import tpu as pltpu
from jax.sharding import PartitionSpec as P

STEP_SIZE = 0.2
SPRING = 4.0
EPSILON = 1e-06
TENSOR_ROWS = ((0, 3, 4), (3, 1, 5), (4, 5, 2))
G = 128
HALF = G // 2
SLABS = 16
PLANES = G // SLABS
PARTS = 2
ROWS = PLANES // PARTS * 8
BLOCK = SLABS * ROWS
MESH = pl.DeviceIdType.MESH
F32 = jnp.float32
BF16 = jnp.bfloat16


def pair(matrix):
    high = matrix.astype(BF16)
    low = (matrix - high.astype(np.float64)).astype(BF16)
    return np.stack([high, low])


def tables():
    index = np.arange(G)
    angle = 2.0 * math.pi * (np.outer(index, index) % G) / G
    cos, sin = np.cos(angle), np.sin(angle)
    z_there = np.concatenate([cos[:, :HALF], cos[:, HALF : HALF + 1], -sin[:, 1:HALF]], axis=1)
    z_back = np.concatenate(
        [cos[:1], 2.0 * cos[1:HALF], cos[HALF : HALF + 1], -2.0 * sin[1:HALF]], axis=0
    )
    order = index.reshape(SLABS, PARTS, PLANES // PARTS).transpose(1, 0, 2).reshape(-1)
    y_there = np.concatenate([cos[order], sin[order]], axis=0)
    y_back = np.concatenate([cos[:, order], -sin[:, order]], axis=1)
    x_there = np.concatenate([cos, sin], axis=1)
    x_back = np.concatenate([cos, -sin], axis=1)
    upper, edge = order > HALF, (order == 0) | (order == HALF)
    middle = ~upper & ~edge
    there = np.zeros((4, G, G), np.float32)
    there[0] = 1.0
    there[3, :, :HALF], there[3, :, HALF:] = -1.0, 1.0
    there[0, upper, 0] = 0.0
    there[0, ~edge, HALF] = 0.0
    there[1, upper, HALF] = 1.0
    there[2, upper, HALF] = -1.0
    there[3, :, HALF] = 0.0
    there[3, ~middle, 0] = 0.0
    back = np.zeros((4, G, G), np.float32)
    back[0] = 1.0
    back[3, :, :HALF], back[3, :, HALF:] = -1.0, 1.0
    back[0, :, 0] = np.where(edge, 1.0, np.where(middle, 2.0, 0.0))
    back[0, :, HALF] = np.where(edge, 1.0, 0.0)
    back[1, :, 0] = np.where(upper, 2.0, 0.0)
    back[2, :, HALF] = np.where(upper, 2.0, 0.0)
    back[3, :, HALF] = np.where(middle, 2.0, 0.0)
    back[3, :, 0] = 0.0
    return (
        pair(z_there),
        pair(y_there),
        pair(x_there),
        pair(x_back),
        pair(y_back),
        pair(z_back),
        there,
        back,
    )


def dot(left, right):
    return jnp.dot(left, right, preferred_element_type=F32)


def split(values):
    high = values.astype(BF16)
    return high, (values - high.astype(F32)).astype(BF16)


def by_left(table, values):
    high, low = split(values)
    return dot(table[0], high) + (dot(table[0], low) + dot(table[1], high))


def by_right(values, table):
    high, low = split(values)
    return dot(high, table[0]) + (dot(low, table[0]) + dot(high, table[1]))


def turned(values):
    return pltpu.roll(values, HALF, 1)


def angle(sine, cosine):
    size = jnp.abs(cosine)
    small, large = jnp.minimum(sine, size), jnp.maximum(sine, size)
    far = small > 0.41421356 * large
    top = jnp.where(far, small - large, small)
    bottom = jnp.where(far, small + large, large)
    ratio = top / jnp.where(large == 0.0, 1.0, bottom)
    square = ratio * ratio
    series = 8.05374449538e-2 * square - 1.38776856032e-1
    series = series * square + 1.99777106478e-1
    series = series * square - 3.33329491539e-1
    value = series * square * ratio + ratio
    value = value + jnp.where(far, math.pi / 4, 0.0)
    value = jnp.where(sine > size, math.pi / 2 - value, value)
    return jnp.where(cosine < 0.0, math.pi - value, value)


def squared_angle(first, second):
    cross_x = first[1] * second[2] - first[2] * second[1]
    cross_y = first[2] * second[0] - first[0] * second[2]
    cross_z = first[0] * second[1] - first[1] * second[0]
    sine = jnp.sqrt(cross_x * cross_x + cross_y * cross_y + cross_z * cross_z)
    cosine = first[0] * second[0] + first[1] * second[1] + first[2] * second[2]
    value = angle(sine, cosine)
    return value * value


def tile_sum(values):
    return jnp.sum(values.reshape(G // 8, 8, G), axis=0)


def row_sum(values):
    return jnp.sum(values, axis=0, keepdims=True)


def whole_sum(values):
    return jnp.sum(jnp.sum(values, axis=0, keepdims=True), axis=1, keepdims=True)


def kernel(
    moment_in,
    labels_in,
    tensor_in,
    anisotropy,
    stiffness,
    z_there,
    y_there,
    x_there,
    x_back,
    y_back,
    z_back,
    there,
    back,
    path_out,
    force_out,
    moment,
    labels,
    tensor,
    packed,
    sending,
    spectrum,
    answer,
    arrived,
    preceding,
    following,
    tangent,
    field,
    path,
    force,
    sums_sent,
    sums,
    load_sem,
    there_sent,
    there_got,
    back_sent,
    back_got,
    halo_sent,
    halo_got,
    image_sent,
    image_got,
    sums_out,
    sums_got,
    store_sem,
):
    image, slab = lax.axis_index("image"), lax.axis_index("space")
    images = lax.axis_size("image")
    other = lax.rem(image + images // 2, images)
    has_preceding, has_following = image > 0, image < images - 1
    next_slab, last_slab = lax.rem(slab + 1, SLABS), lax.rem(slab + SLABS - 1, SLABS)

    def device(of_image, of_slab):
        return {"image": of_image, "space": of_slab}

    barrier = pltpu.get_barrier_semaphore()

    @pl.loop(0, SLABS)
    def _(step):
        pl.semaphore_signal(barrier, inc=1, device_id=device(other, step), device_id_type=MESH)

    @pl.loop(1, SLABS)
    def _(step):
        target = lax.rem(slab + step, SLABS)
        pl.semaphore_signal(barrier, inc=1, device_id=device(image, target), device_id_type=MESH)

    @pl.when(has_preceding)
    def _():
        pl.semaphore_signal(barrier, inc=1, device_id=device(image - 1, slab), device_id_type=MESH)

    @pl.when(has_following)
    def _():
        pl.semaphore_signal(barrier, inc=1, device_id=device(image + 1, slab), device_id_type=MESH)

    loads = [
        pltpu.make_async_copy(
            moment_in.at[0, c], moment.at[c, pl.ds(1, PLANES)], load_sem.at[c]
        )
        for c in range(3)
    ]
    tensor_load = pltpu.make_async_copy(tensor_in, tensor, load_sem.at[3])
    labels_load = pltpu.make_async_copy(labels_in, labels, load_sem.at[4])
    for load in loads:
        load.start()
    tensor_load.start()
    labels_load.start()

    @pl.when(jnp.logical_not(has_preceding))
    def _():
        preceding[...] = jnp.zeros_like(preceding)

    @pl.when(jnp.logical_not(has_following))
    def _():
        following[...] = jnp.zeros_like(following)

    def send_there(c, part):
        @pl.loop(0, SLABS)
        def _(step):
            target = lax.rem(slab + step, SLABS)
            pltpu.make_async_remote_copy(
                src_ref=sending.at[c, pl.ds(part * BLOCK + target * ROWS, ROWS)],
                dst_ref=spectrum.at[c, part, slab],
                send_sem=there_sent.at[c, part],
                recv_sem=there_got.at[c, part],
                device_id=device(other, target),
                device_id_type=MESH,
            ).start()

    def send_back(c, part):
        @pl.loop(0, SLABS)
        def _(step):
            target = lax.rem(slab + step, SLABS)
            pltpu.make_async_remote_copy(
                src_ref=answer.at[c, part, target],
                dst_ref=arrived.at[c, pl.ds(part * BLOCK + slab * ROWS, ROWS)],
                send_sem=back_sent.at[c, part],
                recv_sem=back_got.at[c, part],
                device_id=device(other, target),
                device_id_type=MESH,
            ).start()

    def whole_there(c, part):
        return pltpu.make_async_copy(
            sending.at[c, pl.ds(part * BLOCK, BLOCK)],
            sending.at[c, pl.ds(part * BLOCK, BLOCK)],
            there_sent.at[c, part],
        )

    def whole_spectrum(c, part):
        return pltpu.make_async_copy(
            spectrum.at[c, part], spectrum.at[c, part], there_got.at[c, part]
        )

    def whole_back(c, part):
        return pltpu.make_async_copy(
            answer.at[c, part], answer.at[c, part], back_sent.at[c, part]
        )

    def whole_arrived(c, part):
        return pltpu.make_async_copy(
            arrived.at[c, pl.ds(part * BLOCK, BLOCK)],
            arrived.at[c, pl.ds(part * BLOCK, BLOCK)],
            back_got.at[c, part],
        )

    for c in range(3):
        loads[c].wait()

        @pl.loop(0, PLANES // 2)
        def _(step):
            cells = moment[c, pl.ds(1 + 2 * step, 2)].reshape(2 * G, G)
            lines = by_right(cells, z_there)
            both = by_left(y_there, jnp.concatenate([lines[:G], lines[G:]], axis=1))
            for j in range(2):
                cosine, sine = both[:G, j * G : (j + 1) * G], both[G:, j * G : (j + 1) * G]
                values = there[0] * cosine + there[2] * sine
                values = values + turned(there[1] * cosine + there[3] * sine)
                sending[c, pl.ds(2 * step + j, G, stride=8), :] = values

        if c == 0:
            pl.semaphore_wait(
                barrier, 2 * SLABS - 1 + has_preceding.astype(jnp.int32) + has_following.astype(jnp.int32)
            )
        send_there(c, 0)

    for part in range(1, PARTS):
        for c in range(3):
            send_there(c, part)

    halo = [
        pltpu.make_async_remote_copy(
            src_ref=moment.at[:, source],
            dst_ref=moment.at[:, target],
            send_sem=halo_sent.at[n],
            recv_sem=halo_got.at[n],
            device_id=device(image, to),
            device_id_type=MESH,
        )
        for n, (source, target, to) in enumerate(
            ((PLANES, 0, next_slab), (1, PLANES + 1, last_slab))
        )
    ]
    for copy in halo:
        copy.start()
    own = moment.at[:, pl.ds(1, PLANES)]
    to_following = pltpu.make_async_remote_copy(
        src_ref=own,
        dst_ref=preceding,
        send_sem=image_sent.at[0],
        recv_sem=image_got.at[0],
        device_id=device(lax.rem(image + 1, images), slab),
        device_id_type=MESH,
    )
    to_preceding = pltpu.make_async_remote_copy(
        src_ref=own,
        dst_ref=following,
        send_sem=image_sent.at[1],
        recv_sem=image_got.at[1],
        device_id=device(lax.rem(image + images - 1, images), slab),
        device_id_type=MESH,
    )

    @pl.when(has_following)
    def _():
        to_following.start()

    @pl.when(has_preceding)
    def _():
        to_preceding.start()

    tensor_load.wait()
    lane = lax.broadcasted_iota(jnp.int32, (G, G), 1)

    @pl.loop(0, PLANES)
    def _(row):
        wave = slab * PLANES + row
        first = jnp.logical_and(lane == 0, wave <= HALF)
        middle = jnp.logical_and(lane == HALF, jnp.logical_or(wave == 0, wave >= HALF))
        plain = jnp.logical_and(lane > 0, lane < HALF)
        keep = jnp.logical_or(jnp.logical_or(first, middle), plain)
        for n in range(6):
            values = tensor[n, pl.ds(row, G, stride=8), :]
            packed[n, row] = jnp.where(keep, values, turned(values)) * (-1.0 / G**3)

    labels_load.wait()
    for copy in halo:
        copy.wait()

    @pl.loop(0, PLANES)
    def _(plane):
        region = labels[plane]
        stiff_cell = jnp.zeros((G, G), F32)
        anis_cell = jnp.zeros((G, G), F32)
        for n in range(8):
            stiff_cell = jnp.where(region == n, stiffness[n], stiff_cell)
            anis_cell = jnp.where(region == n, anisotropy[n], anis_cell)
        for c in range(3):
            here = moment[c, plane + 1]
            around = moment[c, plane] + moment[c, plane + 2] - 6.0 * here
            around = around + pltpu.roll(here, 1, 0) + pltpu.roll(here, G - 1, 0)
            around = around + pltpu.roll(here, 1, 1) + pltpu.roll(here, G - 1, 1)
            value = stiff_cell * around
            if c == 2:
                value = value + 2.0 * anis_cell * here
            field[c, plane] = value

    real_column = jnp.logical_and(lane % HALF == 0, lax.rem(slab, SLABS // 2) == 0)
    sign = jnp.where(lane < HALF, 1.0, -1.0)

    def multiply(part):
        for c in range(3):
            whole_spectrum(c, part).wait()

        def row_of(row, first):
            def partner(values, factor):
                result = sign * turned(values)
                if first:
                    result = jnp.where(real_column, factor * values, result)
                return result

            at = pl.ds(pl.multiple_of(row * 8, 8), 8)
            lines = [spectrum[c, part, :, at, :].reshape(G, G) for c in range(3)]
            stack = jnp.concatenate(
                [jnp.concatenate([v, partner(v, 1.0)], axis=0) for v in lines], axis=1
            )
            waves = by_left(x_there, stack)
            waves = [waves[:, b * G : (b + 1) * G] for b in range(3)]
            at_row = part * (PLANES // PARTS) + row
            products = []
            for n in TENSOR_ROWS:
                value = packed[n[0], at_row] * waves[0]
                value = value + packed[n[1], at_row] * waves[1]
                products.append(value + packed[n[2], at_row] * waves[2])
            stack = jnp.concatenate(
                [jnp.concatenate([v, partner(v, -1.0)], axis=0) for v in products], axis=1
            )
            result = by_left(x_back, stack)
            for c in range(3):
                answer[c, part, :, at, :] = result[:, c * G : (c + 1) * G].reshape(SLABS, 8, G)

        first = part == 0
        if first:
            row_of(0, True)

        @pl.loop(1 if first else 0, PLANES // PARTS)
        def _(row):
            row_of(row, False)

        for c in range(3):
            send_back(c, part)

    multiply(0)

    @pl.when(has_preceding)
    def _():
        to_following.wait_recv()

    @pl.when(has_following)
    def _():
        to_preceding.wait_recv()

    def tangent_step(plane, carry):
        here = [moment[c, plane + 1] for c in range(3)]
        before = [preceding[c, plane] for c in range(3)]
        after = [following[c, plane] for c in range(3)]
        change = [after[c] - before[c] for c in range(3)]
        along = change[0] * here[0] + change[1] * here[1] + change[2] * here[2]
        change = [change[c] - along * here[c] for c in range(3)]
        for c in range(3):
            tangent[c, plane] = change[c]
        size = change[0] * change[0] + change[1] * change[1] + change[2] * change[2]
        return (
            carry[0] + tile_sum(size),
            carry[1] + tile_sum(squared_angle(here, after)),
            carry[2] + tile_sum(squared_angle(before, here)),
        )

    zero = jnp.zeros((8, G), F32)
    totals = lax.fori_loop(0, PLANES, tangent_step, (zero, zero, zero))

    def spread(n):
        @pl.loop(1, SLABS)
        def _(step):
            pltpu.make_async_remote_copy(
                src_ref=sums_sent.at[n],
                dst_ref=sums.at[n, step - 1],
                send_sem=sums_out.at[n],
                recv_sem=sums_got.at[n],
                device_id=device(image, lax.rem(slab + step, SLABS)),
                device_id_type=MESH,
            ).start()

    def collect(n):
        pltpu.make_async_copy(sums.at[n], sums.at[n], sums_got.at[n]).wait()
        return sums_sent[n] + jnp.sum(sums[n], axis=0)

    row = lax.broadcasted_iota(jnp.int32, (8, G), 0)
    rows = [jnp.broadcast_to(row_sum(value), (8, G)) for value in totals]
    sums_sent[0] = jnp.where(row == 0, rows[0], jnp.where(row == 1, rows[1], rows[2]))
    spread(0)

    for part in range(1, PARTS):
        multiply(part)

    for c in range(3):
        for part in range(PARTS):
            whole_arrived(c, part).wait()

        @pl.loop(0, PLANES // 2)
        def _(step):
            stack = []
            for j in range(2):
                values = arrived[c, pl.ds(2 * step + j, G, stride=8), :]
                first = back[0] * values + turned(back[1] * values)
                second = back[2] * values + turned(back[3] * values)
                stack.append(jnp.concatenate([first, second], axis=0))
            lines = by_left(y_back, jnp.concatenate(stack, axis=1))
            cells = by_right(jnp.concatenate([lines[:, :G], lines[:, G:]], axis=0), z_back)
            at = pl.ds(2 * step, 2)
            field[c, at] = field[c, at] + cells.reshape(2, G, G)

    def slope_step(plane, carry):
        here = [moment[c, plane + 1] for c in range(3)]
        gradient = [-field[c, plane] for c in range(3)]
        along = gradient[0] * here[0] + gradient[1] * here[1] + gradient[2] * here[2]
        total = jnp.zeros((G, G), F32)
        for c in range(3):
            value = gradient[c] - along * here[c]
            field[c, plane] = value
            total = total + value * tangent[c, plane]
        return carry + tile_sum(total)

    sums_sent[1] = lax.fori_loop(0, PLANES, slope_step, zero)
    spread(1)
    cells = float(G**3)
    first_sums = collect(0)
    parts = [whole_sum(jnp.where(row == n, first_sums, 0.0)) for n in range(3)]
    slope_sum = whole_sum(collect(1))
    factor = jnp.sqrt(cells / (parts[0] + EPSILON))
    spring = SPRING * (jnp.sqrt(parts[1] / cells) - jnp.sqrt(parts[2] / cells))
    strength = (slope_sum * factor / cells + spring) * factor
    movable = jnp.where(jnp.logical_and(has_preceding, has_following), 1.0, 0.0)

    stores = []

    def final_step(plane, carry):
        stepped = []
        for c in range(3):
            value = movable * (strength * tangent[c, plane] - field[c, plane])
            force[c, plane] = value
            stepped.append(moment[c, plane + 1] + STEP_SIZE * value)
        size = stepped[0] * stepped[0] + stepped[1] * stepped[1] + stepped[2] * stepped[2]
        scale = lax.rsqrt(size)
        for c in range(3):
            path[c, plane] = stepped[c] * scale
        return carry

    chunk = PLANES // 4
    for n in range(4):
        lax.fori_loop(n * chunk, (n + 1) * chunk, final_step, 0)
        at = pl.ds(n * chunk, chunk)
        stores.append(
            pltpu.make_async_copy(path.at[:, at], path_out.at[0, :, at], store_sem.at[0, n])
        )
        stores.append(
            pltpu.make_async_copy(force.at[:, at], force_out.at[0, :, at], store_sem.at[1, n])
        )
        stores[-2].start()
        stores[-1].start()

    for part in range(PARTS):
        for c in range(3):
            whole_there(c, part).wait()
            whole_back(c, part).wait()

    @pl.when(has_following)
    def _():
        to_following.wait_send()

    @pl.when(has_preceding)
    def _():
        to_preceding.wait_send()

    for n in range(2):
        out = pltpu.make_async_copy(sums.at[n], sums.at[n], sums_out.at[n])
        out.wait()
    for store in stores:
        store.wait()


def local(magnetization, region_labels, demag_kernel, anisotropy, stiffness):
    block = (3, PLANES, G, G)
    shape = jax.ShapeDtypeStruct((1,) + block, F32)
    any_spec = pl.BlockSpec(memory_space=pl.ANY)
    smem_spec = pl.BlockSpec(memory_space=pltpu.SMEM)
    vmem_spec = pl.BlockSpec(memory_space=pltpu.VMEM)
    constants = [jnp.asarray(table) for table in tables()]
    dma = pltpu.SemaphoreType.DMA
    return pl.pallas_call(
        kernel,
        out_shape=(shape, shape),
        in_specs=[any_spec] * 3 + [smem_spec] * 2 + [vmem_spec] * len(constants),
        out_specs=(any_spec, any_spec),
        scratch_shapes=[
            pltpu.VMEM((3, PLANES + 2, G, G), F32),
            pltpu.VMEM((PLANES, G, G), jnp.int32),
            pltpu.VMEM((6, G * PLANES, G), F32),
            pltpu.VMEM((6, PLANES, G, G), F32),
            pltpu.VMEM((3, PARTS * BLOCK, G), F32),
            pltpu.VMEM((3, PARTS, SLABS, ROWS, G), F32),
            pltpu.VMEM((3, PARTS, SLABS, ROWS, G), F32),
            pltpu.VMEM((3, PARTS * BLOCK, G), F32),
            pltpu.VMEM(block, F32),
            pltpu.VMEM(block, F32),
            pltpu.VMEM(block, F32),
            pltpu.VMEM(block, F32),
            pltpu.VMEM(block, F32),
            pltpu.VMEM(block, F32),
            pltpu.VMEM((2, 8, G), F32),
            pltpu.VMEM((2, SLABS - 1, 8, G), F32),
            dma((5,)),
            dma((3, PARTS)),
            dma((3, PARTS)),
            dma((3, PARTS)),
            dma((3, PARTS)),
            dma((2,)),
            dma((2,)),
            dma((2,)),
            dma((2,)),
            dma((2,)),
            dma((2,)),
            dma((2, 4)),
        ],
        compiler_params=pltpu.CompilerParams(
            collective_id=0, has_side_effects=True, vmem_limit_bytes=48 * 2**20
        ),
    )(
        magnetization,
        region_labels,
        demag_kernel.reshape(6, G * PLANES, G),
        anisotropy,
        stiffness,
        *constants,
    )


def solution(mesh):
    in_specs = (
        P("image", None, "space", None, None),
        P("space", None, None),
        P(None, None, "space", None),
        P(),
        P(),
    )
    out_specs = (P("image", None, "space", None, None), P("image", None, "space", None, None))
    return jax.shard_map(local, mesh=mesh, in_specs=in_specs, out_specs=out_specs, check_vma=False)
```

```python
import functools
import math

import jax
import jax.numpy as jnp
import numpy as np
from jax import lax
from jax.experimental import pallas as pl
from jax.experimental.pallas import tpu as pltpu
from jax.sharding import PartitionSpec as P

STEP_SIZE = 0.2
SPRING = 4.0
EPSILON = 1e-06
TENSOR_ROWS = ((0, 3, 4), (3, 1, 5), (4, 5, 2))
G = 128
HALF = G // 2
SLABS = 16
PLANES = G // SLABS
PARTS = 2
ROWS = PLANES // PARTS * 8
BLOCK = SLABS * ROWS
RELAYS = 3
COLUMN = 4
DEPTH = SLABS // COLUMN
MESH = pl.DeviceIdType.MESH
F32 = jnp.float32
BF16 = jnp.bfloat16


def pair(matrix):
    high = matrix.astype(BF16)
    low = (matrix - high.astype(np.float64)).astype(BF16)
    return np.stack([high, low])


def tables():
    index = np.arange(G)
    angle = 2.0 * math.pi * (np.outer(index, index) % G) / G
    cos, sin = np.cos(angle), np.sin(angle)
    z_there = np.concatenate([cos[:, :HALF], cos[:, HALF : HALF + 1], -sin[:, 1:HALF]], axis=1)
    z_back = np.concatenate(
        [cos[:1], 2.0 * cos[1:HALF], cos[HALF : HALF + 1], -2.0 * sin[1:HALF]], axis=0
    )
    order = index.reshape(SLABS, PARTS, PLANES // PARTS).transpose(1, 0, 2).reshape(-1)
    y_there = np.concatenate([cos[order], sin[order]], axis=0)
    y_back = np.concatenate([cos[:, order], -sin[:, order]], axis=0)
    x_there = np.concatenate([cos, sin], axis=0)
    x_back = np.concatenate([cos, -sin], axis=0)
    upper, edge = order > HALF, (order == 0) | (order == HALF)
    middle = ~upper & ~edge
    there = np.zeros((4, G, G), np.float32)
    there[0] = 1.0
    there[3, :, :HALF], there[3, :, HALF:] = -1.0, 1.0
    there[0, upper, 0] = 0.0
    there[0, ~edge, HALF] = 0.0
    there[1, upper, HALF] = 1.0
    there[2, upper, HALF] = -1.0
    there[3, :, HALF] = 0.0
    there[3, ~middle, 0] = 0.0
    back = np.zeros((4, G, G), np.float32)
    back[0] = 1.0
    back[3, :, :HALF], back[3, :, HALF:] = -1.0, 1.0
    back[0, :, 0] = np.where(edge, 1.0, np.where(middle, 2.0, 0.0))
    back[0, :, HALF] = np.where(edge, 1.0, 0.0)
    back[1, :, 0] = np.where(upper, 2.0, 0.0)
    back[2, :, HALF] = np.where(upper, 2.0, 0.0)
    back[3, :, HALF] = np.where(middle, 2.0, 0.0)
    back[3, :, 0] = 0.0
    return (
        pair(z_there),
        pair(y_there),
        there,
        pair(x_there),
        pair(x_back),
        pair(y_back),
        pair(z_back),
        back,
    )


def dot(left, right):
    return jnp.dot(left, right, preferred_element_type=F32)


def split(values):
    high = values.astype(BF16)
    return high, (values - high.astype(F32)).astype(BF16)


def beside(table):
    return [jnp.concatenate([table[n, :G], table[n, G:]], axis=1) for n in range(2)]


def by_left(table, values):
    high, low = split(values)
    return dot(table[0], high) + (dot(table[0], low) + dot(table[1], high))


def by_right(values, table):
    high, low = split(values)
    return dot(high, table[0]) + (dot(low, table[0]) + dot(high, table[1]))


def turned(values):
    return pltpu.roll(values, HALF, 1)


def angle(sine, cosine):
    size = jnp.abs(cosine)
    small, large = jnp.minimum(sine, size), jnp.maximum(sine, size)
    far = small > 0.41421356 * large
    top = jnp.where(far, small - large, small)
    bottom = jnp.where(far, small + large, large)
    ratio = top / jnp.where(large == 0.0, 1.0, bottom)
    square = ratio * ratio
    series = 8.05374449538e-2 * square - 1.38776856032e-1
    series = series * square + 1.99777106478e-1
    series = series * square - 3.33329491539e-1
    value = series * square * ratio + ratio
    value = value + jnp.where(far, math.pi / 4, 0.0)
    value = jnp.where(sine > size, math.pi / 2 - value, value)
    return jnp.where(cosine < 0.0, math.pi - value, value)


def squared_angle(first, second):
    cross_x = first[1] * second[2] - first[2] * second[1]
    cross_y = first[2] * second[0] - first[0] * second[2]
    cross_z = first[0] * second[1] - first[1] * second[0]
    sine = jnp.sqrt(cross_x * cross_x + cross_y * cross_y + cross_z * cross_z)
    cosine = first[0] * second[0] + first[1] * second[1] + first[2] * second[2]
    value = angle(sine, cosine)
    return value * value


def tile_sum(values):
    return jnp.sum(values.reshape(G // 8, 8, G), axis=0)


def row_sum(values):
    return jnp.sum(values, axis=0, keepdims=True)


def whole_sum(values):
    return jnp.sum(jnp.sum(values, axis=0, keepdims=True), axis=1, keepdims=True)


def kernel(
    moment_in,
    labels_in,
    tensor_in,
    anisotropy_in,
    stiffness_in,
    z_there_in,
    y_there_in,
    there_in,
    x_there_in,
    x_back_in,
    y_back_in,
    z_back_in,
    back_in,
    path_out,
    force_out,
    anisotropy,
    stiffness,
    z_there,
    y_there,
    there,
    x_there,
    x_back,
    y_back,
    z_back,
    back,
    moment,
    labels,
    tensor,
    packed,
    sending,
    spectrum,
    answer,
    arrived,
    preceding,
    following,
    tangent,
    field,
    path,
    force,
    relay,
    relay_halo,
    sums_sent,
    sums,
    load_sem,
    there_sent,
    there_got,
    back_sent,
    back_got,
    halo_sent,
    halo_got,
    image_sent,
    image_got,
    relay_sent,
    relay_got,
    sums_out,
    sums_got,
    store_sem,
):
    image, slab = lax.axis_index("image"), lax.axis_index("space")
    images = lax.axis_size("image")
    other = lax.rem(image + images // 2, images)
    has_preceding, has_following = image > 0, image < images - 1
    next_slab, last_slab = lax.rem(slab + 1, SLABS), lax.rem(slab + SLABS - 1, SLABS)

    def device(of_image, of_slab):
        return {"image": of_image, "space": of_slab}

    barrier = pltpu.get_barrier_semaphore()

    @pl.loop(0, SLABS)
    def _(step):
        pl.semaphore_signal(barrier, inc=1, device_id=device(other, step), device_id_type=MESH)

    @pl.loop(1, SLABS)
    def _(step):
        target = lax.rem(slab + step, SLABS)
        pl.semaphore_signal(barrier, inc=1, device_id=device(image, target), device_id_type=MESH)

    @pl.when(has_preceding)
    def _():
        pl.semaphore_signal(barrier, inc=1, device_id=device(image - 1, slab), device_id_type=MESH)

    @pl.when(has_following)
    def _():
        pl.semaphore_signal(barrier, inc=1, device_id=device(image + 1, slab), device_id_type=MESH)

    middle = images // 2
    left_end, right_end = image == middle - 1, image == middle
    is_end = jnp.logical_or(left_end, right_end)
    left_relay = jnp.logical_and(image < middle - 1, lax.rem(image, 2) == 1)
    right_relay = jnp.logical_and(image > middle, lax.rem(image, 2) == 0)
    is_relay = jnp.logical_or(left_relay, right_relay)

    @pl.when(is_end)
    def _():
        for n in range(RELAYS):
            for target in (2 * n + 1, middle + 2 * n + 2):
                pl.semaphore_signal(
                    barrier, inc=1, device_id=device(target, slab), device_id_type=MESH
                )

    @pl.when(is_relay)
    def _():
        for target in (middle - 1, middle):
            pl.semaphore_signal(
                barrier, inc=1, device_id=device(target, slab), device_id_type=MESH
            )

    loads = [
        pltpu.make_async_copy(
            moment_in.at[0, c], moment.at[c, pl.ds(1, PLANES)], load_sem.at[c]
        )
        for c in range(3)
    ]
    tensor_load = pltpu.make_async_copy(tensor_in, tensor, load_sem.at[3])
    labels_load = pltpu.make_async_copy(labels_in, labels, load_sem.at[4])
    early = [
        pltpu.make_async_copy(source, target, load_sem.at[5 + n])
        for n, (source, target) in enumerate(
            ((z_there_in, z_there), (y_there_in, y_there), (there_in, there))
        )
    ]
    late = [
        pltpu.make_async_copy(source, target, load_sem.at[8 + n])
        for n, (source, target) in enumerate(
            (
                (x_there_in, x_there),
                (x_back_in, x_back),
                (y_back_in, y_back),
                (z_back_in, z_back),
                (back_in, back),
                (anisotropy_in, anisotropy),
                (stiffness_in, stiffness),
            )
        )
    ]
    for load in loads[:1] + early + loads[1:] + [tensor_load] + late + [labels_load]:
        load.start()

    @pl.when(jnp.logical_not(has_preceding))
    def _():
        preceding[...] = jnp.zeros_like(preceding)

    @pl.when(jnp.logical_not(has_following))
    def _():
        following[...] = jnp.zeros_like(following)

    def send_there(c, part):
        @pl.loop(0, SLABS)
        def _(step):
            target = lax.rem(slab + step, SLABS)
            pltpu.make_async_remote_copy(
                src_ref=sending.at[c, pl.ds(part * BLOCK + target * ROWS, ROWS)],
                dst_ref=spectrum.at[c, part, slab],
                send_sem=there_sent.at[c, part],
                recv_sem=there_got.at[c, part],
                device_id=device(other, target),
                device_id_type=MESH,
            ).start()

    def send_back(c, part):
        @pl.loop(0, SLABS)
        def _(step):
            target = lax.rem(slab + step, SLABS)
            pltpu.make_async_remote_copy(
                src_ref=answer.at[c, part, target],
                dst_ref=arrived.at[c, pl.ds(part * BLOCK + slab * ROWS, ROWS)],
                send_sem=back_sent.at[c, part],
                recv_sem=back_got.at[c, part],
                device_id=device(other, target),
                device_id_type=MESH,
            ).start()

    def whole_there(c, part):
        return pltpu.make_async_copy(
            sending.at[c, pl.ds(part * BLOCK, BLOCK)],
            sending.at[c, pl.ds(part * BLOCK, BLOCK)],
            there_sent.at[c, part],
        )

    def whole_spectrum(c, part):
        return pltpu.make_async_copy(
            spectrum.at[c, part], spectrum.at[c, part], there_got.at[c, part]
        )

    def whole_back(c, part):
        return pltpu.make_async_copy(
            answer.at[c, part], answer.at[c, part], back_sent.at[c, part]
        )

    def whole_arrived(c, part):
        return pltpu.make_async_copy(
            arrived.at[c, pl.ds(part * BLOCK, BLOCK)],
            arrived.at[c, pl.ds(part * BLOCK, BLOCK)],
            back_got.at[c, part],
        )

    def remote(source, target, sent, got, of_image, of_slab):
        return pltpu.make_async_remote_copy(
            src_ref=source,
            dst_ref=target,
            send_sem=sent,
            recv_sem=got,
            device_id=device(of_image, of_slab),
            device_id_type=MESH,
        )

    high, low = slab // COLUMN, lax.rem(slab, COLUMN)
    next_high, last_high = lax.rem(high + 1, DEPTH), lax.rem(high + DEPTH - 1, DEPTH)
    at_top, at_bottom = low == COLUMN - 1, low == 0
    strip = G // COLUMN

    def strip_of(plane, n):
        return moment.at[:, plane, pl.ds(n * strip, strip)]

    up_whole = remote(
        moment.at[:, PLANES], moment.at[:, 0], halo_sent.at[0], halo_got.at[0], image, next_slab
    )
    down_whole = remote(
        moment.at[:, 1], moment.at[:, PLANES + 1], halo_sent.at[1], halo_got.at[1], image, last_slab
    )
    up_relay = remote(
        relay_halo.at[0],
        moment.at[:, 0, pl.ds(low * strip, strip)],
        relay_sent.at[1],
        halo_got.at[0],
        image,
        next_high * COLUMN,
    )
    down_relay = remote(
        relay_halo.at[1],
        moment.at[:, PLANES + 1, pl.ds(low * strip, strip)],
        relay_sent.at[2],
        halo_got.at[1],
        image,
        last_high * COLUMN + COLUMN - 1,
    )
    own = moment.at[:, pl.ds(1, PLANES)]
    to_following = remote(
        own, preceding, image_sent.at[0], image_got.at[0], lax.rem(image + 1, images), slab
    )
    to_preceding = remote(
        own, following, image_sent.at[1], image_got.at[1], lax.rem(image + images - 1, images), slab
    )
    share = PLANES // (RELAYS + 1)
    quarter = lax.rem(image, middle) // 2
    right_forward = remote(
        relay,
        preceding.at[:, pl.ds(quarter * share, share)],
        relay_sent.at[0],
        image_got.at[0],
        middle,
        slab,
    )
    left_forward = remote(
        relay,
        following.at[:, pl.ds(quarter * share, share)],
        relay_sent.at[0],
        image_got.at[1],
        middle - 1,
        slab,
    )

    def quarter_of(n):
        return moment.at[:, pl.ds(1 + n * share, share)]

    def send_near():
        @pl.when(left_end)
        def _():
            for n in range(RELAYS):
                remote(
                    quarter_of(n), relay, image_sent.at[0], relay_got.at[0], 2 * n + 1, slab
                ).start()
            remote(
                quarter_of(RELAYS),
                preceding.at[:, pl.ds(RELAYS * share, share)],
                image_sent.at[0],
                image_got.at[0],
                middle,
                slab,
            ).start()

        @pl.when(right_end)
        def _():
            for n in range(1, RELAYS + 1):
                remote(
                    quarter_of(n), relay, image_sent.at[1], relay_got.at[0], middle + 2 * n, slab
                ).start()
            remote(
                quarter_of(0),
                following.at[:, pl.ds(0, share)],
                image_sent.at[1],
                image_got.at[1],
                middle - 1,
                slab,
            ).start()

        @pl.when(at_top)
        def _():
            for n in range(COLUMN - 1):
                remote(
                    strip_of(PLANES, n),
                    relay_halo.at[0],
                    halo_sent.at[0],
                    relay_got.at[1],
                    image,
                    high * COLUMN + n,
                ).start()
            remote(
                strip_of(PLANES, COLUMN - 1),
                strip_of(0, COLUMN - 1),
                halo_sent.at[0],
                halo_got.at[0],
                image,
                next_high * COLUMN,
            ).start()

        @pl.when(at_bottom)
        def _():
            for n in range(1, COLUMN):
                remote(
                    strip_of(1, n),
                    relay_halo.at[1],
                    halo_sent.at[1],
                    relay_got.at[2],
                    image,
                    high * COLUMN + n,
                ).start()
            remote(
                strip_of(1, 0),
                strip_of(PLANES + 1, 0),
                halo_sent.at[1],
                halo_got.at[1],
                image,
                last_high * COLUMN + COLUMN - 1,
            ).start()

        @pl.when(jnp.logical_not(at_top))
        def _():
            up_whole.start()

        @pl.when(jnp.logical_not(at_bottom))
        def _():
            down_whole.start()

        @pl.when(jnp.logical_and(has_following, jnp.logical_not(left_end)))
        def _():
            to_following.start()

        @pl.when(jnp.logical_and(has_preceding, jnp.logical_not(right_end)))
        def _():
            to_preceding.start()

    def forward_relays():
        @pl.when(jnp.logical_not(at_top))
        def _():
            pltpu.make_async_copy(relay_halo.at[0], relay_halo.at[0], relay_got.at[1]).wait()
            up_relay.start()

        @pl.when(jnp.logical_not(at_bottom))
        def _():
            pltpu.make_async_copy(relay_halo.at[1], relay_halo.at[1], relay_got.at[2]).wait()
            down_relay.start()

        @pl.when(left_relay)
        def _():
            pltpu.make_async_copy(relay, relay, relay_got.at[0]).wait()
            right_forward.start()

        @pl.when(right_relay)
        def _():
            pltpu.make_async_copy(relay, relay, relay_got.at[0]).wait()
            left_forward.start()

    for c in range(3):
        if c == 0:
            for load in [loads[0]] + early:
                load.wait()

        @pl.loop(0, PLANES // 2)
        def _(step):
            cells = moment[c, pl.ds(1 + 2 * step, 2)].reshape(2 * G, G)
            lines = by_right(cells, z_there)
            both = by_left(y_there, jnp.concatenate([lines[:G], lines[G:]], axis=1))
            for j in range(2):
                cosine, sine = both[:G, j * G : (j + 1) * G], both[G:, j * G : (j + 1) * G]
                values = there[0] * cosine + there[2] * sine
                values = values + turned(there[1] * cosine + there[3] * sine)
                sending[c, pl.ds(2 * step + j, G, stride=8), :] = values

        if c == 0:
            signals = 2 * SLABS - 1 + has_preceding.astype(jnp.int32)
            signals = signals + has_following.astype(jnp.int32) + 2 * is_relay.astype(jnp.int32)
            pl.semaphore_wait(barrier, signals + 2 * RELAYS * is_end.astype(jnp.int32))
        send_there(c, 0)
        if c == 0:
            for load in loads[1:]:
                load.wait()
            send_near()

    for part in range(1, PARTS):
        for c in range(3):
            send_there(c, part)

    forward_relays()

    tensor_load.wait()
    for load in late:
        load.wait()
    lane = lax.broadcasted_iota(jnp.int32, (G, G), 1)

    @pl.loop(0, PLANES)
    def _(row):
        wave = slab * PLANES + row
        first = jnp.logical_and(lane == 0, wave <= HALF)
        middle = jnp.logical_and(lane == HALF, jnp.logical_or(wave == 0, wave >= HALF))
        plain = jnp.logical_and(lane > 0, lane < HALF)
        keep = jnp.logical_or(jnp.logical_or(first, middle), plain)
        for n in range(6):
            values = tensor[n, pl.ds(row, G, stride=8), :]
            packed[n, row] = jnp.where(keep, values, turned(values)) * (-1.0 / G**3)

    real_column = jnp.logical_and(lane % HALF == 0, lax.rem(slab, SLABS // 2) == 0)
    sign = jnp.where(lane < HALF, 1.0, -1.0)

    def multiply(part):
        for c in range(3):
            whole_spectrum(c, part).wait()

        def row_of(row, first):
            def partner(values, factor):
                result = sign * turned(values)
                if first:
                    result = jnp.where(real_column, factor * values, result)
                return result

            at = pl.ds(pl.multiple_of(row * 8, 8), 8)
            lines = [spectrum[c, part, :, at, :].reshape(G, G) for c in range(3)]
            stack = jnp.concatenate(
                [jnp.concatenate([v, partner(v, 1.0)], axis=0) for v in lines], axis=1
            )
            waves = by_left(beside(x_there), stack)
            waves = [waves[:, b * G : (b + 1) * G] for b in range(3)]
            at_row = part * (PLANES // PARTS) + row
            products = []
            for n in TENSOR_ROWS:
                value = packed[n[0], at_row] * waves[0]
                value = value + packed[n[1], at_row] * waves[1]
                products.append(value + packed[n[2], at_row] * waves[2])
            stack = jnp.concatenate(
                [jnp.concatenate([v, partner(v, -1.0)], axis=0) for v in products], axis=1
            )
            result = by_left(beside(x_back), stack)
            for c in range(3):
                answer[c, part, :, at, :] = result[:, c * G : (c + 1) * G].reshape(SLABS, 8, G)

        first = part == 0
        if first:
            row_of(0, True)

        @pl.loop(1 if first else 0, PLANES // PARTS)
        def _(row):
            row_of(row, False)

        for c in range(3):
            send_back(c, part)

    for part in range(PARTS):
        multiply(part)

    labels_load.wait()
    up_whole.wait_recv()
    down_whole.wait_recv()

    @pl.loop(0, PLANES)
    def _(plane):
        region = labels[plane]
        stiff_cell = jnp.zeros((G, G), F32)
        anis_cell = jnp.zeros((G, G), F32)
        for n in range(8):
            stiff_cell = jnp.where(region == n, stiffness[n], stiff_cell)
            anis_cell = jnp.where(region == n, anisotropy[n], anis_cell)
        for c in range(3):
            here = moment[c, plane + 1]
            around = moment[c, plane] + moment[c, plane + 2] - 6.0 * here
            around = around + pltpu.roll(here, 1, 0) + pltpu.roll(here, G - 1, 0)
            around = around + pltpu.roll(here, 1, 1) + pltpu.roll(here, G - 1, 1)
            value = stiff_cell * around
            if c == 2:
                value = value + 2.0 * anis_cell * here
            field[c, plane] = value

    @pl.when(has_preceding)
    def _():
        to_following.wait_recv()

    @pl.when(has_following)
    def _():
        to_preceding.wait_recv()

    def tangent_step(plane, carry):
        here = [moment[c, plane + 1] for c in range(3)]
        before = [preceding[c, plane] for c in range(3)]
        after = [following[c, plane] for c in range(3)]
        change = [after[c] - before[c] for c in range(3)]
        along = change[0] * here[0] + change[1] * here[1] + change[2] * here[2]
        change = [change[c] - along * here[c] for c in range(3)]
        for c in range(3):
            tangent[c, plane] = change[c]
        size = change[0] * change[0] + change[1] * change[1] + change[2] * change[2]
        return (
            carry[0] + tile_sum(size),
            carry[1] + tile_sum(squared_angle(here, after)),
            carry[2] + tile_sum(squared_angle(before, here)),
        )

    zero = jnp.zeros((8, G), F32)
    totals = lax.fori_loop(0, PLANES, tangent_step, (zero, zero, zero))

    def spread(n):
        @pl.loop(1, SLABS)
        def _(step):
            pltpu.make_async_remote_copy(
                src_ref=sums_sent.at[n],
                dst_ref=sums.at[n, step - 1],
                send_sem=sums_out.at[n],
                recv_sem=sums_got.at[n],
                device_id=device(image, lax.rem(slab + step, SLABS)),
                device_id_type=MESH,
            ).start()

    def collect(n):
        pltpu.make_async_copy(sums.at[n], sums.at[n], sums_got.at[n]).wait()
        return sums_sent[n] + jnp.sum(sums[n], axis=0)

    row = lax.broadcasted_iota(jnp.int32, (8, G), 0)
    rows = [jnp.broadcast_to(row_sum(value), (8, G)) for value in totals]
    sums_sent[0] = jnp.where(row == 0, rows[0], jnp.where(row == 1, rows[1], rows[2]))
    spread(0)

    for c in range(3):
        for part in range(PARTS):
            whole_arrived(c, part).wait()

        @pl.loop(0, PLANES // 2)
        def _(step):
            stack = []
            for j in range(2):
                values = arrived[c, pl.ds(2 * step + j, G, stride=8), :]
                first = back[0] * values + turned(back[1] * values)
                second = back[2] * values + turned(back[3] * values)
                stack.append(jnp.concatenate([first, second], axis=0))
            lines = by_left(beside(y_back), jnp.concatenate(stack, axis=1))
            cells = by_right(jnp.concatenate([lines[:, :G], lines[:, G:]], axis=0), z_back)
            at = pl.ds(2 * step, 2)
            field[c, at] = field[c, at] + cells.reshape(2, G, G)

    def slope_step(plane, carry):
        here = [moment[c, plane + 1] for c in range(3)]
        gradient = [-field[c, plane] for c in range(3)]
        along = gradient[0] * here[0] + gradient[1] * here[1] + gradient[2] * here[2]
        total = jnp.zeros((G, G), F32)
        for c in range(3):
            value = gradient[c] - along * here[c]
            field[c, plane] = value
            total = total + value * tangent[c, plane]
        return carry + tile_sum(total)

    sums_sent[1] = lax.fori_loop(0, PLANES, slope_step, zero)
    spread(1)
    cells = float(G**3)
    first_sums = collect(0)
    parts = [whole_sum(jnp.where(row == n, first_sums, 0.0)) for n in range(3)]
    slope_sum = whole_sum(collect(1))
    factor = jnp.sqrt(cells / (parts[0] + EPSILON))
    spring = SPRING * (jnp.sqrt(parts[1] / cells) - jnp.sqrt(parts[2] / cells))
    strength = (slope_sum * factor / cells + spring) * factor
    movable = jnp.where(jnp.logical_and(has_preceding, has_following), 1.0, 0.0)

    stores = []

    def final_step(plane, carry):
        stepped = []
        for c in range(3):
            value = movable * (strength * tangent[c, plane] - field[c, plane])
            force[c, plane] = value
            stepped.append(moment[c, plane + 1] + STEP_SIZE * value)
        size = stepped[0] * stepped[0] + stepped[1] * stepped[1] + stepped[2] * stepped[2]
        scale = lax.rsqrt(size)
        for c in range(3):
            path[c, plane] = stepped[c] * scale
        return carry

    chunk = PLANES // 4
    for n in range(4):
        lax.fori_loop(n * chunk, (n + 1) * chunk, final_step, 0)
        at = pl.ds(n * chunk, chunk)
        stores.append(
            pltpu.make_async_copy(path.at[:, at], path_out.at[0, :, at], store_sem.at[0, n])
        )
        stores.append(
            pltpu.make_async_copy(force.at[:, at], force_out.at[0, :, at], store_sem.at[1, n])
        )
        stores[-2].start()
        stores[-1].start()

    for part in range(PARTS):
        for c in range(3):
            whole_there(c, part).wait()
            whole_back(c, part).wait()

    up_whole.wait_send()
    down_whole.wait_send()

    @pl.when(jnp.logical_not(at_top))
    def _():
        up_relay.wait_send()

    @pl.when(jnp.logical_not(at_bottom))
    def _():
        down_relay.wait_send()

    @pl.when(left_relay)
    def _():
        right_forward.wait_send()

    @pl.when(right_relay)
    def _():
        left_forward.wait_send()

    @pl.when(has_following)
    def _():
        to_following.wait_send()

    @pl.when(has_preceding)
    def _():
        to_preceding.wait_send()

    for n in range(2):
        out = pltpu.make_async_copy(sums.at[n], sums.at[n], sums_out.at[n])
        out.wait()
    for store in stores:
        store.wait()


def local(magnetization, region_labels, demag_kernel, anisotropy, stiffness):
    block = (3, PLANES, G, G)
    shape = jax.ShapeDtypeStruct((1,) + block, F32)
    hbm_spec = pl.BlockSpec(memory_space=pltpu.HBM)
    constants = [jnp.asarray(table) for table in tables()]
    dma = pltpu.SemaphoreType.DMA
    return pl.pallas_call(
        kernel,
        out_shape=(shape, shape),
        in_specs=[hbm_spec] * (5 + len(constants)),
        out_specs=(hbm_spec, hbm_spec),
        scratch_shapes=[
            pltpu.SMEM((8,), F32),
            pltpu.SMEM((8,), F32),
            *(pltpu.VMEM(table.shape, table.dtype) for table in constants),
            pltpu.VMEM((3, PLANES + 2, G, G), F32),
            pltpu.VMEM((PLANES, G, G), jnp.int32),
            pltpu.VMEM((6, G * PLANES, G), F32),
            pltpu.VMEM((6, PLANES, G, G), F32),
            pltpu.VMEM((3, PARTS * BLOCK, G), F32),
            pltpu.VMEM((3, PARTS, SLABS, ROWS, G), F32),
            pltpu.VMEM((3, PARTS, SLABS, ROWS, G), F32),
            pltpu.VMEM((3, PARTS * BLOCK, G), F32),
            pltpu.VMEM(block, F32),
            pltpu.VMEM(block, F32),
            pltpu.VMEM(block, F32),
            pltpu.VMEM(block, F32),
            pltpu.VMEM(block, F32),
            pltpu.VMEM(block, F32),
            pltpu.VMEM((3, PLANES // (RELAYS + 1), G, G), F32),
            pltpu.VMEM((2, 3, G // COLUMN, G), F32),
            pltpu.VMEM((2, 8, G), F32),
            pltpu.VMEM((2, SLABS - 1, 8, G), F32),
            dma((15,)),
            dma((3, PARTS)),
            dma((3, PARTS)),
            dma((3, PARTS)),
            dma((3, PARTS)),
            dma((2,)),
            dma((2,)),
            dma((2,)),
            dma((2,)),
            dma((3,)),
            dma((3,)),
            dma((2,)),
            dma((2,)),
            dma((2, 4)),
        ],
        compiler_params=pltpu.CompilerParams(
            collective_id=0, has_side_effects=True, vmem_limit_bytes=63 * 2**20
        ),
    )(
        magnetization,
        region_labels,
        demag_kernel.reshape(6, G * PLANES, G),
        anisotropy,
        stiffness,
        *constants,
    )


def solution(mesh):
    in_specs = (
        P("image", None, "space", None, None),
        P("space", None, None),
        P(None, None, "space", None),
        P(),
        P(),
    )
    out_specs = (P("image", None, "space", None, None), P("image", None, "space", None, None))
    return jax.shard_map(local, mesh=mesh, in_specs=in_specs, out_specs=out_specs, check_vma=False)
```

```python
import functools
import math

import jax
import jax.numpy as jnp
import numpy as np
from jax import lax
from jax.experimental import pallas as pl
from jax.experimental.pallas import tpu as pltpu
from jax.sharding import PartitionSpec as P

STEP_SIZE = 0.2
SPRING = 4.0
EPSILON = 1e-06
TENSOR_ROWS = ((0, 3, 4), (3, 1, 5), (4, 5, 2))
G = 128
HALF = G // 2
SLABS = 16
PLANES = G // SLABS
PARTS = 2
ROWS = PLANES // PARTS * 8
BLOCK = SLABS * ROWS
RELAYS = 3
STEPS = 4
STEP_LIMIT = 24
COLUMN = 4
DEPTH = SLABS // COLUMN
MESH = pl.DeviceIdType.MESH
F32 = jnp.float32
BF16 = jnp.bfloat16


def pair(matrix):
    high = matrix.astype(BF16)
    low = (matrix - high.astype(np.float64)).astype(BF16)
    return np.stack([high, low])


def square(matrix):
    high, low = pair(matrix)
    return np.stack([np.concatenate([high, high]), np.concatenate([low, 0 * low])])


def tables():
    index = np.arange(G)
    angle = 2.0 * math.pi * (np.outer(index, index) % G) / G
    cos, sin = np.cos(angle), np.sin(angle)
    z_there = np.concatenate([cos[:, :HALF], cos[:, HALF : HALF + 1], -sin[:, 1:HALF]], axis=1)
    z_back = np.concatenate(
        [cos[:1], 2.0 * cos[1:HALF], cos[HALF : HALF + 1], -2.0 * sin[1:HALF]], axis=0
    )
    order = index.reshape(SLABS, PARTS, PLANES // PARTS).transpose(1, 0, 2).reshape(-1)
    y_there = np.concatenate([cos[order], sin[order]], axis=0)
    y_back = np.concatenate([cos[:, order], -sin[:, order]], axis=0)
    x_there = np.concatenate([cos, sin], axis=0)
    x_back = np.concatenate([cos, -sin], axis=0)
    upper, edge = order > HALF, (order == 0) | (order == HALF)
    middle = ~upper & ~edge
    there = np.zeros((4, G, G), np.float32)
    there[0] = 1.0
    there[3, :, :HALF], there[3, :, HALF:] = -1.0, 1.0
    there[0, upper, 0] = 0.0
    there[0, ~edge, HALF] = 0.0
    there[1, upper, HALF] = 1.0
    there[2, upper, HALF] = -1.0
    there[3, :, HALF] = 0.0
    there[3, ~middle, 0] = 0.0
    back = np.zeros((4, G, G), np.float32)
    back[0] = 1.0
    back[3, :, :HALF], back[3, :, HALF:] = -1.0, 1.0
    back[0, :, 0] = np.where(edge, 1.0, np.where(middle, 2.0, 0.0))
    back[0, :, HALF] = np.where(edge, 1.0, 0.0)
    back[1, :, 0] = np.where(upper, 2.0, 0.0)
    back[2, :, HALF] = np.where(upper, 2.0, 0.0)
    back[3, :, HALF] = np.where(middle, 2.0, 0.0)
    back[3, :, 0] = 0.0
    return (
        square(z_there),
        pair(y_there),
        there,
        pair(x_there),
        pair(x_back),
        pair(y_back),
        square(z_back),
        back,
    )


def dot(left, right):
    return jnp.dot(left, right, preferred_element_type=F32)


def split(values):
    high = values.astype(BF16)
    return high, (values - high.astype(F32)).astype(BF16)


def beside(table):
    return [jnp.concatenate([table[n, :G], table[n, G:]], axis=1) for n in range(2)]


def by_left(table, values):
    rows = table[0].shape[0]
    high, low = split(values)
    both = dot(jnp.concatenate([table[0], table[1]], axis=0), high)
    return both[:rows] + (dot(table[0], low) + both[rows:])


def by_right(values, table):
    both = dot(
        jnp.concatenate(split(values), axis=1), jnp.concatenate([table[0], table[1]], axis=1)
    )
    return both[:, :G] + both[:, G:]


def turned(values):
    return pltpu.roll(values, HALF, 1)


def angle(sine, cosine):
    size = jnp.abs(cosine)
    small, large = jnp.minimum(sine, size), jnp.maximum(sine, size)
    far = small > 0.41421356 * large
    top = jnp.where(far, small - large, small)
    bottom = jnp.where(far, small + large, large)
    ratio = top / jnp.where(large == 0.0, 1.0, bottom)
    square = ratio * ratio
    series = 8.05374449538e-2 * square - 1.38776856032e-1
    series = series * square + 1.99777106478e-1
    series = series * square - 3.33329491539e-1
    value = series * square * ratio + ratio
    value = value + jnp.where(far, math.pi / 4, 0.0)
    value = jnp.where(sine > size, math.pi / 2 - value, value)
    return jnp.where(cosine < 0.0, math.pi - value, value)


def squared_angle(first, second):
    cross_x = first[1] * second[2] - first[2] * second[1]
    cross_y = first[2] * second[0] - first[0] * second[2]
    cross_z = first[0] * second[1] - first[1] * second[0]
    sine = jnp.sqrt(cross_x * cross_x + cross_y * cross_y + cross_z * cross_z)
    cosine = first[0] * second[0] + first[1] * second[1] + first[2] * second[2]
    value = angle(sine, cosine)
    return value * value


def tile_sum(values):
    return jnp.sum(values.reshape(G // 8, 8, G), axis=0)


def row_sum(values):
    return jnp.sum(values, axis=0, keepdims=True)


def whole_sum(values):
    return jnp.sum(jnp.sum(values, axis=0, keepdims=True), axis=1, keepdims=True)


def kernel(
    moment_in,
    labels_in,
    tensor_in,
    anisotropy_in,
    stiffness_in,
    z_there_in,
    y_there_in,
    there_in,
    x_there_in,
    x_back_in,
    y_back_in,
    z_back_in,
    back_in,
    field,
    tangent,
    strength_out,
    anisotropy,
    stiffness,
    z_there,
    y_there,
    there,
    x_there,
    x_back,
    y_back,
    z_back,
    back,
    moment,
    labels,
    tensor,
    packed,
    sending,
    spectrum,
    answer,
    arrived,
    preceding,
    following,
    relay,
    relay_halo,
    sums_sent,
    sums,
    slope_sent,
    slopes,
    load_sem,
    there_sent,
    there_got,
    back_sent,
    back_got,
    halo_sent,
    halo_got,
    image_sent,
    image_got,
    relay_sent,
    relay_got,
    sums_out,
    sums_got,
):
    image, slab = lax.axis_index("image"), lax.axis_index("space")
    images = lax.axis_size("image")
    other = lax.rem(image + images // 2, images)
    has_preceding, has_following = image > 0, image < images - 1
    next_slab, last_slab = lax.rem(slab + 1, SLABS), lax.rem(slab + SLABS - 1, SLABS)

    def device(of_image, of_slab):
        return {"image": of_image, "space": of_slab}

    barrier = pltpu.get_barrier_semaphore()

    @pl.loop(0, SLABS)
    def _(step):
        pl.semaphore_signal(barrier, inc=1, device_id=device(other, step), device_id_type=MESH)

    @pl.loop(1, SLABS)
    def _(step):
        target = lax.rem(slab + step, SLABS)
        pl.semaphore_signal(barrier, inc=1, device_id=device(image, target), device_id_type=MESH)

    @pl.when(has_preceding)
    def _():
        pl.semaphore_signal(barrier, inc=1, device_id=device(image - 1, slab), device_id_type=MESH)

    @pl.when(has_following)
    def _():
        pl.semaphore_signal(barrier, inc=1, device_id=device(image + 1, slab), device_id_type=MESH)

    middle = images // 2
    left_end, right_end = image == middle - 1, image == middle
    is_end = jnp.logical_or(left_end, right_end)
    left_relay = jnp.logical_and(image < middle - 1, lax.rem(image, 2) == 1)
    right_relay = jnp.logical_and(image > middle, lax.rem(image, 2) == 0)
    is_relay = jnp.logical_or(left_relay, right_relay)

    @pl.when(is_end)
    def _():
        for n in range(RELAYS):
            for target in (2 * n + 1, middle + 2 * n + 2):
                pl.semaphore_signal(
                    barrier, inc=1, device_id=device(target, slab), device_id_type=MESH
                )

    @pl.when(is_relay)
    def _():
        for target in (middle - 1, middle):
            pl.semaphore_signal(
                barrier, inc=1, device_id=device(target, slab), device_id_type=MESH
            )

    loads = [
        pltpu.make_async_copy(
            moment_in.at[0, c], moment.at[c, pl.ds(1, PLANES)], load_sem.at[c]
        )
        for c in range(3)
    ]
    tensor_load = pltpu.make_async_copy(tensor_in, tensor, load_sem.at[3])
    labels_load = pltpu.make_async_copy(labels_in, labels, load_sem.at[4])
    early = [
        pltpu.make_async_copy(source, target, load_sem.at[5 + n])
        for n, (source, target) in enumerate(
            ((z_there_in, z_there), (y_there_in, y_there), (there_in, there))
        )
    ]
    late = [
        pltpu.make_async_copy(source, target, load_sem.at[8 + n])
        for n, (source, target) in enumerate(
            (
                (x_there_in, x_there),
                (x_back_in, x_back),
                (y_back_in, y_back),
                (z_back_in, z_back),
                (back_in, back),
                (anisotropy_in, anisotropy),
                (stiffness_in, stiffness),
            )
        )
    ]
    for load in loads[:1] + early + loads[1:] + [tensor_load] + late + [labels_load]:
        load.start()

    @pl.when(jnp.logical_not(has_preceding))
    def _():
        preceding[...] = jnp.zeros_like(preceding)

    @pl.when(jnp.logical_not(has_following))
    def _():
        following[...] = jnp.zeros_like(following)

    def send_there(c, part):
        @pl.loop(0, SLABS)
        def _(step):
            target = lax.rem(slab + step, SLABS)
            pltpu.make_async_remote_copy(
                src_ref=sending.at[c, pl.ds(part * BLOCK + target * ROWS, ROWS)],
                dst_ref=spectrum.at[c, part, slab],
                send_sem=there_sent.at[c, part],
                recv_sem=there_got.at[c, part],
                device_id=device(other, target),
                device_id_type=MESH,
            ).start()

    def send_back(c, part):
        @pl.loop(0, SLABS)
        def _(step):
            target = lax.rem(slab + step, SLABS)
            pltpu.make_async_remote_copy(
                src_ref=answer.at[c, part, target],
                dst_ref=arrived.at[c, pl.ds(part * BLOCK + slab * ROWS, ROWS)],
                send_sem=back_sent.at[c, part],
                recv_sem=back_got.at[c, part],
                device_id=device(other, target),
                device_id_type=MESH,
            ).start()

    def whole_there(c, part):
        return pltpu.make_async_copy(
            sending.at[c, pl.ds(part * BLOCK, BLOCK)],
            sending.at[c, pl.ds(part * BLOCK, BLOCK)],
            there_sent.at[c, part],
        )

    def whole_spectrum(c, part):
        return pltpu.make_async_copy(
            spectrum.at[c, part], spectrum.at[c, part], there_got.at[c, part]
        )

    def whole_back(c, part):
        return pltpu.make_async_copy(
            answer.at[c, part], answer.at[c, part], back_sent.at[c, part]
        )

    def whole_arrived(c, part):
        return pltpu.make_async_copy(
            arrived.at[c, pl.ds(part * BLOCK, BLOCK)],
            arrived.at[c, pl.ds(part * BLOCK, BLOCK)],
            back_got.at[c, part],
        )

    def remote(source, target, sent, got, of_image, of_slab):
        return pltpu.make_async_remote_copy(
            src_ref=source,
            dst_ref=target,
            send_sem=sent,
            recv_sem=got,
            device_id=device(of_image, of_slab),
            device_id_type=MESH,
        )

    high, low = slab // COLUMN, lax.rem(slab, COLUMN)
    next_high, last_high = lax.rem(high + 1, DEPTH), lax.rem(high + DEPTH - 1, DEPTH)
    at_top, at_bottom = low == COLUMN - 1, low == 0
    strip = G // COLUMN

    def strip_of(plane, n):
        return moment.at[:, plane, pl.ds(n * strip, strip)]

    up_whole = remote(
        moment.at[:, PLANES], moment.at[:, 0], halo_sent.at[0], halo_got.at[0], image, next_slab
    )
    down_whole = remote(
        moment.at[:, 1], moment.at[:, PLANES + 1], halo_sent.at[1], halo_got.at[1], image, last_slab
    )
    up_relay = remote(
        relay_halo.at[0],
        moment.at[:, 0, pl.ds(low * strip, strip)],
        relay_sent.at[1],
        halo_got.at[0],
        image,
        next_high * COLUMN,
    )
    down_relay = remote(
        relay_halo.at[1],
        moment.at[:, PLANES + 1, pl.ds(low * strip, strip)],
        relay_sent.at[2],
        halo_got.at[1],
        image,
        last_high * COLUMN + COLUMN - 1,
    )
    own = moment.at[:, pl.ds(1, PLANES)]
    to_following = remote(
        own, preceding, image_sent.at[0], image_got.at[0], lax.rem(image + 1, images), slab
    )
    to_preceding = remote(
        own, following, image_sent.at[1], image_got.at[1], lax.rem(image + images - 1, images), slab
    )
    share = PLANES // (RELAYS + 1)
    quarter = lax.rem(image, middle) // 2
    right_forward = remote(
        relay,
        preceding.at[:, pl.ds(quarter * share, share)],
        relay_sent.at[0],
        image_got.at[0],
        middle,
        slab,
    )
    left_forward = remote(
        relay,
        following.at[:, pl.ds(quarter * share, share)],
        relay_sent.at[0],
        image_got.at[1],
        middle - 1,
        slab,
    )

    def quarter_of(n):
        return moment.at[:, pl.ds(1 + n * share, share)]

    def send_near():
        @pl.when(left_end)
        def _():
            for n in range(RELAYS):
                remote(
                    quarter_of(n), relay, image_sent.at[0], relay_got.at[0], 2 * n + 1, slab
                ).start()
            remote(
                quarter_of(RELAYS),
                preceding.at[:, pl.ds(RELAYS * share, share)],
                image_sent.at[0],
                image_got.at[0],
                middle,
                slab,
            ).start()

        @pl.when(right_end)
        def _():
            for n in range(1, RELAYS + 1):
                remote(
                    quarter_of(n), relay, image_sent.at[1], relay_got.at[0], middle + 2 * n, slab
                ).start()
            remote(
                quarter_of(0),
                following.at[:, pl.ds(0, share)],
                image_sent.at[1],
                image_got.at[1],
                middle - 1,
                slab,
            ).start()

        @pl.when(at_top)
        def _():
            for n in range(COLUMN - 1):
                remote(
                    strip_of(PLANES, n),
                    relay_halo.at[0],
                    halo_sent.at[0],
                    relay_got.at[1],
                    image,
                    high * COLUMN + n,
                ).start()
            remote(
                strip_of(PLANES, COLUMN - 1),
                strip_of(0, COLUMN - 1),
                halo_sent.at[0],
                halo_got.at[0],
                image,
                next_high * COLUMN,
            ).start()

        @pl.when(at_bottom)
        def _():
            for n in range(1, COLUMN):
                remote(
                    strip_of(1, n),
                    relay_halo.at[1],
                    halo_sent.at[1],
                    relay_got.at[2],
                    image,
                    high * COLUMN + n,
                ).start()
            remote(
                strip_of(1, 0),
                strip_of(PLANES + 1, 0),
                halo_sent.at[1],
                halo_got.at[1],
                image,
                last_high * COLUMN + COLUMN - 1,
            ).start()

        @pl.when(jnp.logical_not(at_top))
        def _():
            up_whole.start()

        @pl.when(jnp.logical_not(at_bottom))
        def _():
            down_whole.start()

        @pl.when(jnp.logical_and(has_following, jnp.logical_not(left_end)))
        def _():
            to_following.start()

        @pl.when(jnp.logical_and(has_preceding, jnp.logical_not(right_end)))
        def _():
            to_preceding.start()

    def forward_relays():
        @pl.when(jnp.logical_not(at_top))
        def _():
            pltpu.make_async_copy(relay_halo.at[0], relay_halo.at[0], relay_got.at[1]).wait()
            up_relay.start()

        @pl.when(jnp.logical_not(at_bottom))
        def _():
            pltpu.make_async_copy(relay_halo.at[1], relay_halo.at[1], relay_got.at[2]).wait()
            down_relay.start()

        @pl.when(left_relay)
        def _():
            pltpu.make_async_copy(relay, relay, relay_got.at[0]).wait()
            right_forward.start()

        @pl.when(right_relay)
        def _():
            pltpu.make_async_copy(relay, relay, relay_got.at[0]).wait()
            left_forward.start()

    for c in range(3):
        if c == 0:
            for load in [loads[0]] + early:
                load.wait()

        @pl.loop(0, PLANES // 2)
        def _(step):
            cells = moment[c, pl.ds(1 + 2 * step, 2)].reshape(2 * G, G)
            lines = by_right(cells, z_there)
            both = by_left(y_there, jnp.concatenate([lines[:G], lines[G:]], axis=1))
            for j in range(2):
                cosine, sine = both[:G, j * G : (j + 1) * G], both[G:, j * G : (j + 1) * G]
                values = there[0] * cosine + there[2] * sine
                values = values + turned(there[1] * cosine + there[3] * sine)
                sending[c, pl.ds(2 * step + j, G, stride=8), :] = values

        if c == 0:
            signals = 2 * SLABS - 1 + has_preceding.astype(jnp.int32)
            signals = signals + has_following.astype(jnp.int32) + 2 * is_relay.astype(jnp.int32)
            pl.semaphore_wait(barrier, signals + 2 * RELAYS * is_end.astype(jnp.int32))
        send_there(c, 0)
        if c == 0:
            for load in loads[1:]:
                load.wait()
            send_near()

    for part in range(1, PARTS):
        for c in range(3):
            send_there(c, part)

    forward_relays()

    tensor_load.wait()
    for load in late:
        load.wait()
    lane = lax.broadcasted_iota(jnp.int32, (G, G), 1)

    @pl.loop(0, PLANES)
    def _(row):
        wave = slab * PLANES + row
        first = jnp.logical_and(lane == 0, wave <= HALF)
        middle = jnp.logical_and(lane == HALF, jnp.logical_or(wave == 0, wave >= HALF))
        plain = jnp.logical_and(lane > 0, lane < HALF)
        keep = jnp.logical_or(jnp.logical_or(first, middle), plain)
        for n in range(6):
            values = tensor[n, pl.ds(row, G, stride=8), :]
            packed[n, row] = jnp.where(keep, values, turned(values)) * (-1.0 / G**3)

    real_column = jnp.logical_and(lane % HALF == 0, lax.rem(slab, SLABS // 2) == 0)
    sign = jnp.where(lane < HALF, 1.0, -1.0)

    def multiply(part):
        for c in range(3):
            whole_spectrum(c, part).wait()

        def row_of(row, first):
            def partner(values, factor):
                result = sign * turned(values)
                if first:
                    result = jnp.where(real_column, factor * values, result)
                return result

            at = pl.ds(pl.multiple_of(row * 8, 8), 8)
            lines = [spectrum[c, part, :, at, :].reshape(G, G) for c in range(3)]
            stack = jnp.concatenate(
                [jnp.concatenate([v, partner(v, 1.0)], axis=0) for v in lines], axis=1
            )
            waves = by_left(beside(x_there), stack)
            waves = [waves[:, b * G : (b + 1) * G] for b in range(3)]
            at_row = part * (PLANES // PARTS) + row
            products = []
            for n in TENSOR_ROWS:
                value = packed[n[0], at_row] * waves[0]
                value = value + packed[n[1], at_row] * waves[1]
                products.append(value + packed[n[2], at_row] * waves[2])
            stack = jnp.concatenate(
                [jnp.concatenate([v, partner(v, -1.0)], axis=0) for v in products], axis=1
            )
            result = by_left(beside(x_back), stack)
            for c in range(3):
                answer[c, part, :, at, :] = result[:, c * G : (c + 1) * G].reshape(SLABS, 8, G)

        first = part == 0
        if first:
            row_of(0, True)

        @pl.loop(1 if first else 0, PLANES // PARTS)
        def _(row):
            row_of(row, False)

        for c in range(3):
            send_back(c, part)

    for part in range(PARTS):
        multiply(part)

    labels_load.wait()
    up_whole.wait_recv()
    down_whole.wait_recv()

    @pl.loop(0, PLANES)
    def _(plane):
        region = labels[plane]
        stiff_cell = jnp.zeros((G, G), F32)
        anis_cell = jnp.zeros((G, G), F32)
        for n in range(8):
            stiff_cell = jnp.where(region == n, stiffness[n], stiff_cell)
            anis_cell = jnp.where(region == n, anisotropy[n], anis_cell)
        for c in range(3):
            here = moment[c, plane + 1]
            around = moment[c, plane] + moment[c, plane + 2] - 6.0 * here
            around = around + pltpu.roll(here, 1, 0) + pltpu.roll(here, G - 1, 0)
            around = around + pltpu.roll(here, 1, 1) + pltpu.roll(here, G - 1, 1)
            value = stiff_cell * around
            if c == 2:
                value = value + 2.0 * anis_cell * here
            field[c, plane] = value

    @pl.when(has_preceding)
    def _():
        to_following.wait_recv()

    @pl.when(has_following)
    def _():
        to_preceding.wait_recv()

    def tangent_step(plane, carry):
        here = [moment[c, plane + 1] for c in range(3)]
        before = [preceding[c, plane] for c in range(3)]
        after = [following[c, plane] for c in range(3)]
        change = [after[c] - before[c] for c in range(3)]
        along = change[0] * here[0] + change[1] * here[1] + change[2] * here[2]
        change = [change[c] - along * here[c] for c in range(3)]
        for c in range(3):
            tangent[c, plane] = change[c]
        size = change[0] * change[0] + change[1] * change[1] + change[2] * change[2]
        return (
            carry[0] + tile_sum(size),
            carry[1] + tile_sum(squared_angle(here, after)),
            carry[2] + tile_sum(squared_angle(before, here)),
        )

    zero = jnp.zeros((8, G), F32)
    totals = lax.fori_loop(0, PLANES, tangent_step, (zero, zero, zero))

    def spread(source, targets, n):
        @pl.loop(1, SLABS)
        def _(step):
            remote(
                source,
                targets.at[step - 1],
                sums_out.at[n],
                sums_got.at[n],
                image,
                lax.rem(slab + step, SLABS),
            ).start()

    def collect(source, targets, n):
        pltpu.make_async_copy(targets, targets, sums_got.at[n]).wait()
        return source[...] + jnp.sum(targets[...], axis=0)

    row = lax.broadcasted_iota(jnp.int32, (8, G), 0)
    rows = [jnp.broadcast_to(row_sum(value), (8, G)) for value in totals]
    sums_sent[...] = jnp.where(row == 0, rows[0], jnp.where(row == 1, rows[1], rows[2]))
    spread(sums_sent, sums, 0)

    slope = jnp.zeros((1, G), F32)
    for c in range(3):
        for part in range(PARTS):
            whole_arrived(c, part).wait()

        def back_step(step, carry):
            stack = []
            for j in range(2):
                values = arrived[c, pl.ds(2 * step + j, G, stride=8), :]
                first = back[0] * values + turned(back[1] * values)
                second = back[2] * values + turned(back[3] * values)
                stack.append(jnp.concatenate([first, second], axis=0))
            lines = by_left(beside(y_back), jnp.concatenate(stack, axis=1))
            cells = by_right(jnp.concatenate([lines[:, :G], lines[:, G:]], axis=0), z_back)
            at = pl.ds(2 * step, 2)
            whole = field[c, at].reshape(2 * G, G) + cells
            field[c, at] = whole.reshape(2, G, G)
            return carry - row_sum(whole * tangent[c, at].reshape(2 * G, G))

        slope = lax.fori_loop(0, PLANES // 2, back_step, slope)

    slope_sent[...] = slope

    spread(slope_sent, slopes, 1)

    def normal_step(plane, carry):
        here = [moment[c, plane + 1] for c in range(3)]
        gradient = [-field[c, plane] for c in range(3)]
        along = gradient[0] * here[0] + gradient[1] * here[1] + gradient[2] * here[2]
        for c in range(3):
            field[c, plane] = gradient[c] - along * here[c]
        return carry

    lax.fori_loop(0, PLANES, normal_step, 0)
    cells = float(G**3)
    first_sums = collect(sums_sent, sums, 0)
    parts = [whole_sum(jnp.where(row == n, first_sums, 0.0)) for n in range(3)]
    slope_sum = whole_sum(collect(slope_sent, slopes, 1))
    factor = jnp.sqrt(cells / (parts[0] + EPSILON))
    spring = SPRING * (jnp.sqrt(parts[1] / cells) - jnp.sqrt(parts[2] / cells))
    strength = (slope_sum * factor / cells + spring) * factor
    strength_out[...] = jnp.broadcast_to(strength, (1, G))

    for part in range(PARTS):
        for c in range(3):
            whole_there(c, part).wait()
            whole_back(c, part).wait()

    up_whole.wait_send()
    down_whole.wait_send()

    @pl.when(jnp.logical_not(at_top))
    def _():
        up_relay.wait_send()

    @pl.when(jnp.logical_not(at_bottom))
    def _():
        down_relay.wait_send()

    @pl.when(left_relay)
    def _():
        right_forward.wait_send()

    @pl.when(right_relay)
    def _():
        left_forward.wait_send()

    @pl.when(has_following)
    def _():
        to_following.wait_send()

    @pl.when(has_preceding)
    def _():
        to_preceding.wait_send()

    pltpu.make_async_copy(sums, sums, sums_out.at[0]).wait()
    pltpu.make_async_copy(slopes, slopes, sums_out.at[1]).wait()


def step_kernel(
    moment, normal, tangent, strength, path_out, force_out, path, force, store_sem
):
    image = lax.axis_index("image")
    inside = jnp.logical_and(image > 0, image < lax.axis_size("image") - 1)
    movable = jnp.where(inside, 1.0, 0.0)
    chunk = PLANES // STEPS
    stores = []
    factor = strength[...]

    def plane_step(plane, carry):
        stepped = []
        for c in range(3):
            value = movable * (factor * tangent[c, plane] - normal[c, plane])
            force[c, plane] = value
            stepped.append(moment[0, c, plane] + STEP_SIZE * value)
        size = stepped[0] * stepped[0] + stepped[1] * stepped[1] + stepped[2] * stepped[2]
        scale = lax.rsqrt(size)
        for c in range(3):
            path[c, plane] = stepped[c] * scale
        return carry

    for n in range(STEPS):
        lax.fori_loop(n * chunk, (n + 1) * chunk, plane_step, 0)
        at = pl.ds(n * chunk, chunk)
        stores.append(
            pltpu.make_async_copy(path.at[:, at], path_out.at[0, :, at], store_sem.at[0, n])
        )
        stores.append(
            pltpu.make_async_copy(force.at[:, at], force_out.at[0, :, at], store_sem.at[1, n])
        )
        stores[-2].start()
        stores[-1].start()
    for store in stores:
        store.wait()


def local(magnetization, region_labels, demag_kernel, anisotropy, stiffness):
    block = (3, PLANES, G, G)
    shape = jax.ShapeDtypeStruct((1,) + block, F32)
    hbm_spec = pl.BlockSpec(memory_space=pltpu.HBM)
    vmem_spec = pl.BlockSpec(memory_space=pltpu.VMEM)

    def in_hbm(array):
        return pltpu.with_memory_space_constraint(array, pltpu.HBM)

    constants = [jnp.asarray(table) for table in tables()]
    dma = pltpu.SemaphoreType.DMA
    normal, tangent, strength = pl.pallas_call(
        kernel,
        out_shape=(
            pltpu.VMEM(block, F32),
            pltpu.VMEM(block, F32),
            pltpu.VMEM((1, G), F32),
        ),
        in_specs=[hbm_spec] * (5 + len(constants)),
        out_specs=(vmem_spec, vmem_spec, vmem_spec),
        scratch_shapes=[
            pltpu.SMEM((8,), F32),
            pltpu.SMEM((8,), F32),
            *(pltpu.VMEM(table.shape, table.dtype) for table in constants),
            pltpu.VMEM((3, PLANES + 2, G, G), F32),
            pltpu.VMEM((PLANES, G, G), jnp.int32),
            pltpu.VMEM((6, G * PLANES, G), F32),
            pltpu.VMEM((6, PLANES, G, G), F32),
            pltpu.VMEM((3, PARTS * BLOCK, G), F32),
            pltpu.VMEM((3, PARTS, SLABS, ROWS, G), F32),
            pltpu.VMEM((3, PARTS, SLABS, ROWS, G), F32),
            pltpu.VMEM((3, PARTS * BLOCK, G), F32),
            pltpu.VMEM(block, F32),
            pltpu.VMEM(block, F32),
            pltpu.VMEM((3, PLANES // (RELAYS + 1), G, G), F32),
            pltpu.VMEM((2, 3, G // COLUMN, G), F32),
            pltpu.VMEM((8, G), F32),
            pltpu.VMEM((SLABS - 1, 8, G), F32),
            pltpu.VMEM((1, G), F32),
            pltpu.VMEM((SLABS - 1, 1, G), F32),
            dma((15,)),
            dma((3, PARTS)),
            dma((3, PARTS)),
            dma((3, PARTS)),
            dma((3, PARTS)),
            dma((2,)),
            dma((2,)),
            dma((2,)),
            dma((2,)),
            dma((3,)),
            dma((3,)),
            dma((2,)),
            dma((2,)),
        ],
        compiler_params=pltpu.CompilerParams(
            collective_id=0, has_side_effects=True, vmem_limit_bytes=40 * 2**20
        ),
    )(
        in_hbm(magnetization),
        in_hbm(region_labels),
        in_hbm(demag_kernel.reshape(6, G * PLANES, G)),
        in_hbm(anisotropy),
        in_hbm(stiffness),
        *(in_hbm(constant) for constant in constants),
    )
    return pl.pallas_call(
        step_kernel,
        out_shape=(shape, shape),
        in_specs=[vmem_spec] * 4,
        out_specs=(hbm_spec, hbm_spec),
        scratch_shapes=[pltpu.VMEM(block, F32)] * 2 + [dma((2, STEPS))],
        compiler_params=pltpu.CompilerParams(vmem_limit_bytes=STEP_LIMIT * 2**20),
    )(magnetization, normal, tangent, strength)


def solution(mesh):
    in_specs = (
        P("image", None, "space", None, None),
        P("space", None, None),
        P(None, None, "space", None),
        P(),
        P(),
    )
    out_specs = (P("image", None, "space", None, None), P("image", None, "space", None, None))
    return jax.shard_map(local, mesh=mesh, in_specs=in_specs, out_specs=out_specs, check_vma=False)
```

```python
import functools
import math

import jax
import jax.numpy as jnp
import numpy as np
from jax import lax
from jax.experimental import pallas as pl
from jax.experimental.pallas import tpu as pltpu
from jax.sharding import PartitionSpec as P

STEP_SIZE = 0.2
SPRING = 4.0
EPSILON = 1e-06
TENSOR_ROWS = ((0, 3, 4), (3, 1, 5), (4, 5, 2))
G = 128
HALF = G // 2
SLABS = 16
PLANES = G // SLABS
PARTS = 2
ROWS = PLANES // PARTS * 8
BLOCK = SLABS * ROWS
RELAYS = PLANES - 1
STEPS = 8
STEP_LIMIT = 24
COLUMN = 4
DEPTH = SLABS // COLUMN
MESH = pl.DeviceIdType.MESH
F32 = jnp.float32
BF16 = jnp.bfloat16


def pair(matrix):
    high = matrix.astype(BF16)
    low = (matrix - high.astype(np.float64)).astype(BF16)
    return np.stack([high, low])


def square(matrix):
    high, low = pair(matrix)
    return np.stack([np.concatenate([high, high]), np.concatenate([low, 0 * low])])


def tables():
    index = np.arange(G)
    angle = 2.0 * math.pi * (np.outer(index, index) % G) / G
    cos, sin = np.cos(angle), np.sin(angle)
    z_there = np.concatenate([cos[:, :HALF], cos[:, HALF : HALF + 1], -sin[:, 1:HALF]], axis=1)
    z_back = np.concatenate(
        [cos[:1], 2.0 * cos[1:HALF], cos[HALF : HALF + 1], -2.0 * sin[1:HALF]], axis=0
    )
    order = index.reshape(SLABS, PARTS, PLANES // PARTS).transpose(1, 0, 2).reshape(-1)
    y_there = np.concatenate([cos[order], sin[order]], axis=0)
    y_back = np.concatenate([cos[:, order], -sin[:, order]], axis=0)
    x_there = np.concatenate([cos, sin], axis=0)
    x_back = np.concatenate([cos, -sin], axis=0)
    upper, edge = order > HALF, (order == 0) | (order == HALF)
    middle = ~upper & ~edge
    there = np.zeros((4, G, G), np.float32)
    there[0] = 1.0
    there[3, :, :HALF], there[3, :, HALF:] = -1.0, 1.0
    there[0, upper, 0] = 0.0
    there[0, ~edge, HALF] = 0.0
    there[1, upper, HALF] = 1.0
    there[2, upper, HALF] = -1.0
    there[3, :, HALF] = 0.0
    there[3, ~middle, 0] = 0.0
    back = np.zeros((4, G, G), np.float32)
    back[0] = 1.0
    back[3, :, :HALF], back[3, :, HALF:] = -1.0, 1.0
    back[0, :, 0] = np.where(edge, 1.0, np.where(middle, 2.0, 0.0))
    back[0, :, HALF] = np.where(edge, 1.0, 0.0)
    back[1, :, 0] = np.where(upper, 2.0, 0.0)
    back[2, :, HALF] = np.where(upper, 2.0, 0.0)
    back[3, :, HALF] = np.where(middle, 2.0, 0.0)
    back[3, :, 0] = 0.0
    return (
        square(z_there),
        pair(y_there),
        there,
        pair(x_there),
        pair(x_back),
        pair(y_back),
        square(z_back),
        back,
    )


def dot(left, right):
    return jnp.dot(left, right, preferred_element_type=F32)


def split(values):
    high = values.astype(BF16)
    return high, (values - high.astype(F32)).astype(BF16)


def beside(table):
    return [jnp.concatenate([table[n, :G], table[n, G:]], axis=1) for n in range(2)]


def by_left(table, values):
    rows = table[0].shape[0]
    high, low = split(values)
    both = dot(jnp.concatenate([table[0], table[1]], axis=0), high)
    return both[:rows] + (dot(table[0], low) + both[rows:])


def by_right(values, table):
    both = dot(
        jnp.concatenate(split(values), axis=1), jnp.concatenate([table[0], table[1]], axis=1)
    )
    return both[:, :G] + both[:, G:]


def turned(values):
    return pltpu.roll(values, HALF, 1)


def angle(sine, cosine):
    size = jnp.abs(cosine)
    small, large = jnp.minimum(sine, size), jnp.maximum(sine, size)
    far = small > 0.41421356 * large
    top = jnp.where(far, small - large, small)
    bottom = jnp.where(far, small + large, large)
    ratio = top / jnp.where(large == 0.0, 1.0, bottom)
    square = ratio * ratio
    series = 8.05374449538e-2 * square - 1.38776856032e-1
    series = series * square + 1.99777106478e-1
    series = series * square - 3.33329491539e-1
    value = series * square * ratio + ratio
    value = value + jnp.where(far, math.pi / 4, 0.0)
    value = jnp.where(sine > size, math.pi / 2 - value, value)
    return jnp.where(cosine < 0.0, math.pi - value, value)


def squared_angle(first, second):
    cross_x = first[1] * second[2] - first[2] * second[1]
    cross_y = first[2] * second[0] - first[0] * second[2]
    cross_z = first[0] * second[1] - first[1] * second[0]
    sine = jnp.sqrt(cross_x * cross_x + cross_y * cross_y + cross_z * cross_z)
    cosine = first[0] * second[0] + first[1] * second[1] + first[2] * second[2]
    value = angle(sine, cosine)
    return value * value


def tile_sum(values):
    return jnp.sum(values.reshape(G // 8, 8, G), axis=0)


def row_sum(values):
    return jnp.sum(values, axis=0, keepdims=True)


def whole_sum(values):
    return jnp.sum(jnp.sum(values, axis=0, keepdims=True), axis=1, keepdims=True)


def kernel(
    moment_in,
    labels_in,
    tensor_in,
    anisotropy_in,
    stiffness_in,
    z_there_in,
    y_there_in,
    there_in,
    x_there_in,
    x_back_in,
    y_back_in,
    z_back_in,
    back_in,
    field,
    tangent,
    strength_out,
    anisotropy,
    stiffness,
    z_there,
    y_there,
    there,
    x_there,
    x_back,
    y_back,
    z_back,
    back,
    moment,
    labels,
    tensor,
    packed,
    sending,
    spectrum,
    answer,
    arrived,
    preceding,
    following,
    relay,
    relay_halo,
    sums_sent,
    sums,
    slope_sent,
    slopes,
    load_sem,
    there_sent,
    there_got,
    back_sent,
    back_got,
    halo_sent,
    halo_got,
    image_sent,
    image_got,
    relay_sent,
    relay_got,
    sums_out,
    sums_got,
):
    image, slab = lax.axis_index("image"), lax.axis_index("space")
    images = lax.axis_size("image")
    other = lax.rem(image + images // 2, images)
    other = other + 1 - 2 * lax.rem(other, 2)
    has_preceding, has_following = image > 0, image < images - 1
    next_slab, last_slab = lax.rem(slab + 1, SLABS), lax.rem(slab + SLABS - 1, SLABS)

    def device(of_image, of_slab):
        return {"image": of_image, "space": of_slab}

    barrier = pltpu.get_barrier_semaphore()

    @pl.loop(0, SLABS)
    def _(step):
        target = lax.rem(slab + step, SLABS)
        pl.semaphore_signal(barrier, inc=1, device_id=device(other, target), device_id_type=MESH)

    @pl.loop(1, SLABS)
    def _(step):
        target = lax.rem(slab + step, SLABS)
        pl.semaphore_signal(barrier, inc=1, device_id=device(image, target), device_id_type=MESH)

    @pl.when(has_preceding)
    def _():
        pl.semaphore_signal(barrier, inc=1, device_id=device(image - 1, slab), device_id_type=MESH)

    @pl.when(has_following)
    def _():
        pl.semaphore_signal(barrier, inc=1, device_id=device(image + 1, slab), device_id_type=MESH)

    middle = images // 2
    left_end, right_end = image == middle - 1, image == middle
    is_end = jnp.logical_or(left_end, right_end)
    left_relay, right_relay = image < middle - 1, image > middle
    is_relay = jnp.logical_or(left_relay, right_relay)

    @pl.when(is_end)
    def _():
        for n in range(RELAYS):
            for target in (n, middle + n + 1):
                pl.semaphore_signal(
                    barrier, inc=1, device_id=device(target, slab), device_id_type=MESH
                )

    @pl.when(is_relay)
    def _():
        for target in (middle - 1, middle):
            pl.semaphore_signal(
                barrier, inc=1, device_id=device(target, slab), device_id_type=MESH
            )

    loads = [
        pltpu.make_async_copy(
            moment_in.at[0, c], moment.at[c, pl.ds(1, PLANES)], load_sem.at[c]
        )
        for c in range(3)
    ]
    tensor_load = pltpu.make_async_copy(tensor_in, tensor, load_sem.at[3])
    labels_load = pltpu.make_async_copy(labels_in, labels, load_sem.at[4])
    early = [
        pltpu.make_async_copy(source, target, load_sem.at[5 + n])
        for n, (source, target) in enumerate(
            ((z_there_in, z_there), (y_there_in, y_there), (there_in, there))
        )
    ]
    late = [
        pltpu.make_async_copy(source, target, load_sem.at[8 + n])
        for n, (source, target) in enumerate(
            (
                (x_there_in, x_there),
                (x_back_in, x_back),
                (y_back_in, y_back),
                (z_back_in, z_back),
                (back_in, back),
                (anisotropy_in, anisotropy),
                (stiffness_in, stiffness),
            )
        )
    ]
    for load in loads[:1] + early + loads[1:] + [tensor_load] + late + [labels_load]:
        load.start()

    @pl.when(jnp.logical_not(has_preceding))
    def _():
        preceding[...] = jnp.zeros_like(preceding)

    @pl.when(jnp.logical_not(has_following))
    def _():
        following[...] = jnp.zeros_like(following)

    def send_there(c, part):
        @pl.loop(0, SLABS)
        def _(step):
            target = lax.rem(slab + step, SLABS)
            pltpu.make_async_remote_copy(
                src_ref=sending.at[c, pl.ds(part * BLOCK + target * ROWS, ROWS)],
                dst_ref=spectrum.at[c, part, slab],
                send_sem=there_sent.at[c, part],
                recv_sem=there_got.at[c, part],
                device_id=device(other, target),
                device_id_type=MESH,
            ).start()

    def send_back(c, part):
        @pl.loop(0, SLABS)
        def _(step):
            target = lax.rem(slab + step, SLABS)
            pltpu.make_async_remote_copy(
                src_ref=answer.at[c, part, target],
                dst_ref=arrived.at[c, pl.ds(part * BLOCK + slab * ROWS, ROWS)],
                send_sem=back_sent.at[c, part],
                recv_sem=back_got.at[c, part],
                device_id=device(other, target),
                device_id_type=MESH,
            ).start()

    def whole_there(c, part):
        return pltpu.make_async_copy(
            sending.at[c, pl.ds(part * BLOCK, BLOCK)],
            sending.at[c, pl.ds(part * BLOCK, BLOCK)],
            there_sent.at[c, part],
        )

    def whole_spectrum(c, part):
        return pltpu.make_async_copy(
            spectrum.at[c, part], spectrum.at[c, part], there_got.at[c, part]
        )

    def whole_back(c, part):
        return pltpu.make_async_copy(
            answer.at[c, part], answer.at[c, part], back_sent.at[c, part]
        )

    def whole_arrived(c, part):
        return pltpu.make_async_copy(
            arrived.at[c, pl.ds(part * BLOCK, BLOCK)],
            arrived.at[c, pl.ds(part * BLOCK, BLOCK)],
            back_got.at[c, part],
        )

    def remote(source, target, sent, got, of_image, of_slab):
        return pltpu.make_async_remote_copy(
            src_ref=source,
            dst_ref=target,
            send_sem=sent,
            recv_sem=got,
            device_id=device(of_image, of_slab),
            device_id_type=MESH,
        )

    high, low = slab // COLUMN, lax.rem(slab, COLUMN)
    next_high, last_high = lax.rem(high + 1, DEPTH), lax.rem(high + DEPTH - 1, DEPTH)
    at_top, at_bottom = low == COLUMN - 1, low == 0
    strip = G // COLUMN

    def strip_of(plane, n):
        return moment.at[:, plane, pl.ds(n * strip, strip)]

    up_whole = remote(
        moment.at[:, PLANES], moment.at[:, 0], halo_sent.at[0], halo_got.at[0], image, next_slab
    )
    down_whole = remote(
        moment.at[:, 1], moment.at[:, PLANES + 1], halo_sent.at[1], halo_got.at[1], image, last_slab
    )
    up_relay = remote(
        relay_halo.at[0],
        moment.at[:, 0, pl.ds(low * strip, strip)],
        relay_sent.at[1],
        halo_got.at[0],
        image,
        next_high * COLUMN,
    )
    down_relay = remote(
        relay_halo.at[1],
        moment.at[:, PLANES + 1, pl.ds(low * strip, strip)],
        relay_sent.at[2],
        halo_got.at[1],
        image,
        last_high * COLUMN + COLUMN - 1,
    )
    own = moment.at[:, pl.ds(1, PLANES)]
    to_following = remote(
        own, preceding, image_sent.at[0], image_got.at[0], lax.rem(image + 1, images), slab
    )
    to_preceding = remote(
        own, following, image_sent.at[1], image_got.at[1], lax.rem(image + images - 1, images), slab
    )
    share = PLANES // (RELAYS + 1)
    turn = lax.rem(image, middle)
    right_forward = remote(
        relay,
        preceding.at[:, pl.ds(turn * share, share)],
        relay_sent.at[0],
        image_got.at[0],
        middle,
        slab,
    )
    left_forward = remote(
        relay,
        following.at[:, pl.ds(turn * share, share)],
        relay_sent.at[0],
        image_got.at[1],
        middle - 1,
        slab,
    )

    def share_of(n):
        return moment.at[:, pl.ds(1 + n * share, share)]

    def send_near():
        @pl.when(left_end)
        def _():
            for n in range(RELAYS):
                remote(
                    share_of(n), relay, image_sent.at[0], relay_got.at[0], n, slab
                ).start()
            remote(
                share_of(RELAYS),
                preceding.at[:, pl.ds(RELAYS * share, share)],
                image_sent.at[0],
                image_got.at[0],
                middle,
                slab,
            ).start()

        @pl.when(right_end)
        def _():
            for n in range(1, RELAYS + 1):
                remote(
                    share_of(n), relay, image_sent.at[1], relay_got.at[0], middle + n, slab
                ).start()
            remote(
                share_of(0),
                following.at[:, pl.ds(0, share)],
                image_sent.at[1],
                image_got.at[1],
                middle - 1,
                slab,
            ).start()

        @pl.when(at_top)
        def _():
            for n in range(COLUMN - 1):
                remote(
                    strip_of(PLANES, n),
                    relay_halo.at[0],
                    halo_sent.at[0],
                    relay_got.at[1],
                    image,
                    high * COLUMN + n,
                ).start()
            remote(
                strip_of(PLANES, COLUMN - 1),
                strip_of(0, COLUMN - 1),
                halo_sent.at[0],
                halo_got.at[0],
                image,
                next_high * COLUMN,
            ).start()

        @pl.when(at_bottom)
        def _():
            for n in range(1, COLUMN):
                remote(
                    strip_of(1, n),
                    relay_halo.at[1],
                    halo_sent.at[1],
                    relay_got.at[2],
                    image,
                    high * COLUMN + n,
                ).start()
            remote(
                strip_of(1, 0),
                strip_of(PLANES + 1, 0),
                halo_sent.at[1],
                halo_got.at[1],
                image,
                last_high * COLUMN + COLUMN - 1,
            ).start()

        @pl.when(jnp.logical_not(at_top))
        def _():
            up_whole.start()

        @pl.when(jnp.logical_not(at_bottom))
        def _():
            down_whole.start()

        @pl.when(jnp.logical_and(has_following, jnp.logical_not(left_end)))
        def _():
            to_following.start()

        @pl.when(jnp.logical_and(has_preceding, jnp.logical_not(right_end)))
        def _():
            to_preceding.start()

    def forward_strips():
        @pl.when(jnp.logical_not(at_top))
        def _():
            pltpu.make_async_copy(relay_halo.at[0], relay_halo.at[0], relay_got.at[1]).wait()
            up_relay.start()

        @pl.when(jnp.logical_not(at_bottom))
        def _():
            pltpu.make_async_copy(relay_halo.at[1], relay_halo.at[1], relay_got.at[2]).wait()
            down_relay.start()

    def forward_image():
        @pl.when(left_relay)
        def _():
            pltpu.make_async_copy(relay, relay, relay_got.at[0]).wait()
            right_forward.start()

        @pl.when(right_relay)
        def _():
            pltpu.make_async_copy(relay, relay, relay_got.at[0]).wait()
            left_forward.start()

    for c in range(3):
        if c == 0:
            for load in [loads[0]] + early:
                load.wait()

        @pl.loop(0, PLANES // 2)
        def _(step):
            cells = moment[c, pl.ds(1 + 2 * step, 2)].reshape(2 * G, G)
            lines = by_right(cells, z_there)
            both = by_left(y_there, jnp.concatenate([lines[:G], lines[G:]], axis=1))
            for j in range(2):
                cosine, sine = both[:G, j * G : (j + 1) * G], both[G:, j * G : (j + 1) * G]
                values = there[0] * cosine + there[2] * sine
                values = values + turned(there[1] * cosine + there[3] * sine)
                sending[c, pl.ds(2 * step + j, G, stride=8), :] = values

        if c == 0:
            signals = 2 * SLABS - 1 + has_preceding.astype(jnp.int32)
            signals = signals + has_following.astype(jnp.int32) + 2 * is_relay.astype(jnp.int32)
            pl.semaphore_wait(barrier, signals + 2 * RELAYS * is_end.astype(jnp.int32))
        send_there(c, 0)
        if c == 0:
            for load in loads[1:]:
                load.wait()
            send_near()

    for part in range(1, PARTS):
        for c in range(3):
            send_there(c, part)

    forward_strips()

    tensor_load.wait()
    for load in late:
        load.wait()
    lane = lax.broadcasted_iota(jnp.int32, (G, G), 1)

    @pl.loop(0, PLANES)
    def _(row):
        wave = slab * PLANES + row
        first = jnp.logical_and(lane == 0, wave <= HALF)
        middle = jnp.logical_and(lane == HALF, jnp.logical_or(wave == 0, wave >= HALF))
        plain = jnp.logical_and(lane > 0, lane < HALF)
        keep = jnp.logical_or(jnp.logical_or(first, middle), plain)
        for n in range(6):
            values = tensor[n, pl.ds(row, G, stride=8), :]
            packed[n, row] = jnp.where(keep, values, turned(values)) * (-1.0 / G**3)

    real_column = jnp.logical_and(lane % HALF == 0, lax.rem(slab, SLABS // 2) == 0)
    sign = jnp.where(lane < HALF, 1.0, -1.0)

    def multiply(part):
        for c in range(3):
            whole_spectrum(c, part).wait()

        def row_of(row, first):
            def partner(values, factor):
                result = sign * turned(values)
                if first:
                    result = jnp.where(real_column, factor * values, result)
                return result

            at = pl.ds(pl.multiple_of(row * 8, 8), 8)
            lines = [spectrum[c, part, :, at, :].reshape(G, G) for c in range(3)]
            stack = jnp.concatenate(
                [jnp.concatenate([v, partner(v, 1.0)], axis=0) for v in lines], axis=1
            )
            waves = by_left(beside(x_there), stack)
            waves = [waves[:, b * G : (b + 1) * G] for b in range(3)]
            at_row = part * (PLANES // PARTS) + row
            products = []
            for n in TENSOR_ROWS:
                value = packed[n[0], at_row] * waves[0]
                value = value + packed[n[1], at_row] * waves[1]
                products.append(value + packed[n[2], at_row] * waves[2])
            stack = jnp.concatenate(
                [jnp.concatenate([v, partner(v, -1.0)], axis=0) for v in products], axis=1
            )
            result = by_left(beside(x_back), stack)
            for c in range(3):
                answer[c, part, :, at, :] = result[:, c * G : (c + 1) * G].reshape(SLABS, 8, G)

        first = part == 0
        if first:
            row_of(0, True)

        @pl.loop(1 if first else 0, PLANES // PARTS)
        def _(row):
            row_of(row, False)

        for c in range(3):
            send_back(c, part)

    for part in range(PARTS):
        multiply(part)
        if part == 0:
            forward_image()

    labels_load.wait()
    up_whole.wait_recv()
    down_whole.wait_recv()

    @pl.loop(0, PLANES)
    def _(plane):
        region = labels[plane]
        stiff_cell = jnp.zeros((G, G), F32)
        anis_cell = jnp.zeros((G, G), F32)
        for n in range(8):
            stiff_cell = jnp.where(region == n, stiffness[n], stiff_cell)
            anis_cell = jnp.where(region == n, anisotropy[n], anis_cell)
        for c in range(3):
            here = moment[c, plane + 1]
            around = moment[c, plane] + moment[c, plane + 2] - 6.0 * here
            around = around + pltpu.roll(here, 1, 0) + pltpu.roll(here, G - 1, 0)
            around = around + pltpu.roll(here, 1, 1) + pltpu.roll(here, G - 1, 1)
            value = stiff_cell * around
            if c == 2:
                value = value + 2.0 * anis_cell * here
            field[c, plane] = value

    @pl.when(has_preceding)
    def _():
        to_following.wait_recv()

    @pl.when(has_following)
    def _():
        to_preceding.wait_recv()

    def tangent_step(plane, carry):
        here = [moment[c, plane + 1] for c in range(3)]
        before = [preceding[c, plane] for c in range(3)]
        after = [following[c, plane] for c in range(3)]
        change = [after[c] - before[c] for c in range(3)]
        along = change[0] * here[0] + change[1] * here[1] + change[2] * here[2]
        change = [change[c] - along * here[c] for c in range(3)]
        for c in range(3):
            tangent[c, plane] = change[c]
        size = change[0] * change[0] + change[1] * change[1] + change[2] * change[2]
        return (
            carry[0] + tile_sum(size),
            carry[1] + tile_sum(squared_angle(here, after)),
            carry[2] + tile_sum(squared_angle(before, here)),
        )

    zero = jnp.zeros((8, G), F32)
    totals = lax.fori_loop(0, PLANES, tangent_step, (zero, zero, zero))

    def spread(source, targets, n):
        @pl.loop(1, SLABS)
        def _(step):
            remote(
                source,
                targets.at[step - 1],
                sums_out.at[n],
                sums_got.at[n],
                image,
                lax.rem(slab + step, SLABS),
            ).start()

    def collect(source, targets, n):
        pltpu.make_async_copy(targets, targets, sums_got.at[n]).wait()
        return source[...] + jnp.sum(targets[...], axis=0)

    row = lax.broadcasted_iota(jnp.int32, (8, G), 0)
    rows = [jnp.broadcast_to(row_sum(value), (8, G)) for value in totals]
    sums_sent[...] = jnp.where(row == 0, rows[0], jnp.where(row == 1, rows[1], rows[2]))
    spread(sums_sent, sums, 0)

    slope = jnp.zeros((1, G), F32)
    for c in range(3):
        for part in range(PARTS):
            whole_arrived(c, part).wait()

        def back_step(step, carry):
            stack = []
            for j in range(2):
                values = arrived[c, pl.ds(2 * step + j, G, stride=8), :]
                first = back[0] * values + turned(back[1] * values)
                second = back[2] * values + turned(back[3] * values)
                stack.append(jnp.concatenate([first, second], axis=0))
            lines = by_left(beside(y_back), jnp.concatenate(stack, axis=1))
            cells = by_right(jnp.concatenate([lines[:, :G], lines[:, G:]], axis=0), z_back)
            at = pl.ds(2 * step, 2)
            whole = field[c, at].reshape(2 * G, G) + cells
            field[c, at] = whole.reshape(2, G, G)
            return carry - row_sum(whole * tangent[c, at].reshape(2 * G, G))

        slope = lax.fori_loop(0, PLANES // 2, back_step, slope)

    slope_sent[...] = slope

    spread(slope_sent, slopes, 1)

    def normal_step(plane, carry):
        here = [moment[c, plane + 1] for c in range(3)]
        gradient = [-field[c, plane] for c in range(3)]
        along = gradient[0] * here[0] + gradient[1] * here[1] + gradient[2] * here[2]
        for c in range(3):
            field[c, plane] = gradient[c] - along * here[c]
        return carry

    lax.fori_loop(0, PLANES, normal_step, 0)
    cells = float(G**3)
    first_sums = collect(sums_sent, sums, 0)
    parts = [whole_sum(jnp.where(row == n, first_sums, 0.0)) for n in range(3)]
    factor = jnp.sqrt(cells / (parts[0] + EPSILON))
    spring = SPRING * (jnp.sqrt(parts[1] / cells) - jnp.sqrt(parts[2] / cells))
    per_slope, constant = factor * factor / cells, spring * factor
    strength = whole_sum(collect(slope_sent, slopes, 1)) * per_slope + constant
    strength_out[...] = jnp.broadcast_to(strength, (1, G))

    for part in range(PARTS):
        for c in range(3):
            whole_there(c, part).wait()
            whole_back(c, part).wait()

    up_whole.wait_send()
    down_whole.wait_send()

    @pl.when(jnp.logical_not(at_top))
    def _():
        up_relay.wait_send()

    @pl.when(jnp.logical_not(at_bottom))
    def _():
        down_relay.wait_send()

    @pl.when(left_relay)
    def _():
        right_forward.wait_send()

    @pl.when(right_relay)
    def _():
        left_forward.wait_send()

    @pl.when(has_following)
    def _():
        to_following.wait_send()

    @pl.when(has_preceding)
    def _():
        to_preceding.wait_send()

    pltpu.make_async_copy(sums, sums, sums_out.at[0]).wait()
    pltpu.make_async_copy(slopes, slopes, sums_out.at[1]).wait()


def step_kernel(
    moment, normal, tangent, strength, path_out, force_out, path, force, store_sem
):
    image = lax.axis_index("image")
    inside = jnp.logical_and(image > 0, image < lax.axis_size("image") - 1)
    movable = jnp.where(inside, 1.0, 0.0)
    chunk = PLANES // STEPS
    stores = []
    factor = strength[...]

    def plane_step(plane, carry):
        stepped = []
        for c in range(3):
            value = movable * (factor * tangent[c, plane] - normal[c, plane])
            force[c, plane] = value
            stepped.append(moment[0, c, plane] + STEP_SIZE * value)
        size = stepped[0] * stepped[0] + stepped[1] * stepped[1] + stepped[2] * stepped[2]
        scale = lax.rsqrt(size)
        for c in range(3):
            path[c, plane] = stepped[c] * scale
        return carry

    for n in range(STEPS):
        lax.fori_loop(n * chunk, (n + 1) * chunk, plane_step, 0)
        at = pl.ds(n * chunk, chunk)
        stores.append(
            pltpu.make_async_copy(path.at[:, at], path_out.at[0, :, at], store_sem.at[0, n])
        )
        stores.append(
            pltpu.make_async_copy(force.at[:, at], force_out.at[0, :, at], store_sem.at[1, n])
        )
        stores[-2].start()
        stores[-1].start()
    for store in stores:
        store.wait()


def local(magnetization, region_labels, demag_kernel, anisotropy, stiffness):
    block = (3, PLANES, G, G)
    shape = jax.ShapeDtypeStruct((1,) + block, F32)
    hbm_spec = pl.BlockSpec(memory_space=pltpu.HBM)
    vmem_spec = pl.BlockSpec(memory_space=pltpu.VMEM)

    def in_hbm(array):
        return pltpu.with_memory_space_constraint(array, pltpu.HBM)

    constants = [jnp.asarray(table) for table in tables()]
    dma = pltpu.SemaphoreType.DMA
    normal, tangent, strength = pl.pallas_call(
        kernel,
        out_shape=(
            pltpu.VMEM(block, F32),
            pltpu.VMEM(block, F32),
            pltpu.VMEM((1, G), F32),
        ),
        in_specs=[hbm_spec] * (5 + len(constants)),
        out_specs=(vmem_spec, vmem_spec, vmem_spec),
        scratch_shapes=[
            pltpu.SMEM((8,), F32),
            pltpu.SMEM((8,), F32),
            *(pltpu.VMEM(table.shape, table.dtype) for table in constants),
            pltpu.VMEM((3, PLANES + 2, G, G), F32),
            pltpu.VMEM((PLANES, G, G), jnp.int32),
            pltpu.VMEM((6, G * PLANES, G), F32),
            pltpu.VMEM((6, PLANES, G, G), F32),
            pltpu.VMEM((3, PARTS * BLOCK, G), F32),
            pltpu.VMEM((3, PARTS, SLABS, ROWS, G), F32),
            pltpu.VMEM((3, PARTS, SLABS, ROWS, G), F32),
            pltpu.VMEM((3, PARTS * BLOCK, G), F32),
            pltpu.VMEM(block, F32),
            pltpu.VMEM(block, F32),
            pltpu.VMEM((3, PLANES // (RELAYS + 1), G, G), F32),
            pltpu.VMEM((2, 3, G // COLUMN, G), F32),
            pltpu.VMEM((8, G), F32),
            pltpu.VMEM((SLABS - 1, 8, G), F32),
            pltpu.VMEM((1, G), F32),
            pltpu.VMEM((SLABS - 1, 1, G), F32),
            dma((15,)),
            dma((3, PARTS)),
            dma((3, PARTS)),
            dma((3, PARTS)),
            dma((3, PARTS)),
            dma((2,)),
            dma((2,)),
            dma((2,)),
            dma((2,)),
            dma((3,)),
            dma((3,)),
            dma((2,)),
            dma((2,)),
        ],
        compiler_params=pltpu.CompilerParams(
            collective_id=0, has_side_effects=True, vmem_limit_bytes=40 * 2**20
        ),
    )(
        in_hbm(magnetization),
        in_hbm(region_labels),
        in_hbm(demag_kernel.reshape(6, G * PLANES, G)),
        in_hbm(anisotropy),
        in_hbm(stiffness),
        *(in_hbm(constant) for constant in constants),
    )
    return pl.pallas_call(
        step_kernel,
        out_shape=(shape, shape),
        in_specs=[vmem_spec] * 4,
        out_specs=(hbm_spec, hbm_spec),
        scratch_shapes=[pltpu.VMEM(block, F32)] * 2 + [dma((2, STEPS))],
        compiler_params=pltpu.CompilerParams(vmem_limit_bytes=STEP_LIMIT * 2**20),
    )(magnetization, normal, tangent, strength)


def solution(mesh):
    in_specs = (
        P("image", None, "space", None, None),
        P("space", None, None),
        P(None, None, "space", None),
        P(),
        P(),
    )
    out_specs = (P("image", None, "space", None, None), P("image", None, "space", None, None))
    return jax.shard_map(local, mesh=mesh, in_specs=in_specs, out_specs=out_specs, check_vma=False)
```

```python
import functools
import math

import jax
import jax.numpy as jnp
import numpy as np
from jax import lax
from jax.experimental import pallas as pl
from jax.experimental.pallas import tpu as pltpu
from jax.sharding import PartitionSpec as P

STEP_SIZE = 0.2
SPRING = 4.0
EPSILON = 1e-06
TENSOR_ROWS = ((0, 3, 4), (3, 1, 5), (4, 5, 2))
G = 128
HALF = G // 2
SLABS = 16
PLANES = G // SLABS
PARTS = 2
ROWS = PLANES // PARTS * 8
BLOCK = SLABS * ROWS
RELAYS = PLANES - 1
STEPS = 8
STEP_LIMIT = 24
COLUMN = 4
DEPTH = SLABS // COLUMN
MESH = pl.DeviceIdType.MESH
F32 = jnp.float32
BF16 = jnp.bfloat16


def pair(matrix):
    high = matrix.astype(BF16)
    low = (matrix - high.astype(np.float64)).astype(BF16)
    return np.stack([high, low])


def square(matrix):
    high, low = pair(matrix)
    return np.stack([np.concatenate([high, high]), np.concatenate([low, 0 * low])])


def tables():
    index = np.arange(G)
    angle = 2.0 * math.pi * (np.outer(index, index) % G) / G
    cos, sin = np.cos(angle), np.sin(angle)
    z_there = np.concatenate([cos[:, :HALF], cos[:, HALF : HALF + 1], -sin[:, 1:HALF]], axis=1)
    z_back = np.concatenate(
        [cos[:1], 2.0 * cos[1:HALF], cos[HALF : HALF + 1], -2.0 * sin[1:HALF]], axis=0
    )
    order = index.reshape(SLABS, PARTS, PLANES // PARTS).transpose(1, 0, 2).reshape(-1)
    y_there = np.concatenate([cos[order], sin[order]], axis=0)
    y_back = np.concatenate(
        [np.concatenate([cos[:, o], -sin[:, o]], axis=1) for o in order.reshape(PARTS, -1)], axis=0
    )
    x_there = np.concatenate([cos, sin], axis=0)
    x_back = np.concatenate([cos, -sin], axis=0)
    upper, edge = order > HALF, (order == 0) | (order == HALF)
    middle = ~upper & ~edge
    there = np.zeros((4, G, G), np.float32)
    there[0] = 1.0
    there[3, :, :HALF], there[3, :, HALF:] = -1.0, 1.0
    there[0, upper, 0] = 0.0
    there[0, ~edge, HALF] = 0.0
    there[1, upper, HALF] = 1.0
    there[2, upper, HALF] = -1.0
    there[3, :, HALF] = 0.0
    there[3, ~middle, 0] = 0.0
    back = np.zeros((4, G, G), np.float32)
    back[0] = 1.0
    back[3, :, :HALF], back[3, :, HALF:] = -1.0, 1.0
    back[0, :, 0] = np.where(edge, 1.0, np.where(middle, 2.0, 0.0))
    back[0, :, HALF] = np.where(edge, 1.0, 0.0)
    back[1, :, 0] = np.where(upper, 2.0, 0.0)
    back[2, :, HALF] = np.where(upper, 2.0, 0.0)
    back[3, :, HALF] = np.where(middle, 2.0, 0.0)
    back[3, :, 0] = 0.0
    return (
        square(z_there),
        pair(y_there),
        there,
        pair(x_there),
        pair(x_back),
        pair(y_back),
        square(z_back),
        back,
    )


def dot(left, right):
    return jnp.dot(left, right, preferred_element_type=F32)


def split(values):
    high = values.astype(BF16)
    return high, (values - high.astype(F32)).astype(BF16)


def beside(table):
    return [jnp.concatenate([table[n, :G], table[n, G:]], axis=1) for n in range(2)]


def by_left(table, values):
    rows = table[0].shape[0]
    high, low = split(values)
    both = dot(jnp.concatenate([table[0], table[1]], axis=0), high)
    return both[:rows] + (dot(table[0], low) + both[rows:])


def by_right(values, table):
    both = dot(
        jnp.concatenate(split(values), axis=1), jnp.concatenate([table[0], table[1]], axis=1)
    )
    return both[:, :G] + both[:, G:]


def turned(values):
    return pltpu.roll(values, HALF, 1)


def angle(sine, cosine):
    size = jnp.abs(cosine)
    small, large = jnp.minimum(sine, size), jnp.maximum(sine, size)
    far = small > 0.41421356 * large
    top = jnp.where(far, small - large, small)
    bottom = jnp.where(far, small + large, large)
    ratio = top / jnp.where(large == 0.0, 1.0, bottom)
    square = ratio * ratio
    series = 8.05374449538e-2 * square - 1.38776856032e-1
    series = series * square + 1.99777106478e-1
    series = series * square - 3.33329491539e-1
    value = series * square * ratio + ratio
    value = value + jnp.where(far, math.pi / 4, 0.0)
    value = jnp.where(sine > size, math.pi / 2 - value, value)
    return jnp.where(cosine < 0.0, math.pi - value, value)


def squared_angle(first, second):
    cross_x = first[1] * second[2] - first[2] * second[1]
    cross_y = first[2] * second[0] - first[0] * second[2]
    cross_z = first[0] * second[1] - first[1] * second[0]
    sine = jnp.sqrt(cross_x * cross_x + cross_y * cross_y + cross_z * cross_z)
    cosine = first[0] * second[0] + first[1] * second[1] + first[2] * second[2]
    value = angle(sine, cosine)
    return value * value


def tile_sum(values):
    return jnp.sum(values.reshape(G // 8, 8, G), axis=0)


def row_sum(values):
    return jnp.sum(values, axis=0, keepdims=True)


def whole_sum(values):
    return jnp.sum(jnp.sum(values, axis=0, keepdims=True), axis=1, keepdims=True)


def kernel(
    moment_in,
    labels_in,
    tensor_in,
    anisotropy_in,
    stiffness_in,
    z_there_in,
    y_there_in,
    there_in,
    x_there_in,
    x_back_in,
    y_back_in,
    z_back_in,
    back_in,
    field,
    tangent,
    strength_out,
    anisotropy,
    stiffness,
    z_there,
    y_there,
    there,
    x_there,
    x_back,
    y_back,
    z_back,
    back,
    moment,
    labels,
    tensor,
    packed,
    sending,
    spectrum,
    answer,
    arrived,
    preceding,
    following,
    relay,
    relay_halo,
    sums_sent,
    sums,
    slope_sent,
    slopes,
    load_sem,
    there_sent,
    there_got,
    back_sent,
    back_got,
    halo_sent,
    halo_got,
    image_sent,
    image_got,
    relay_sent,
    relay_got,
    sums_out,
    sums_got,
):
    image, slab = lax.axis_index("image"), lax.axis_index("space")
    images = lax.axis_size("image")
    other = lax.rem(image + images // 2, images)
    other = other + 1 - 2 * lax.rem(other, 2)
    has_preceding, has_following = image > 0, image < images - 1
    next_slab, last_slab = lax.rem(slab + 1, SLABS), lax.rem(slab + SLABS - 1, SLABS)

    def device(of_image, of_slab):
        return {"image": of_image, "space": of_slab}

    barrier = pltpu.get_barrier_semaphore()

    @pl.loop(0, SLABS)
    def _(step):
        target = lax.rem(slab + step, SLABS)
        pl.semaphore_signal(barrier, inc=1, device_id=device(other, target), device_id_type=MESH)

    @pl.loop(1, SLABS)
    def _(step):
        target = lax.rem(slab + step, SLABS)
        pl.semaphore_signal(barrier, inc=1, device_id=device(image, target), device_id_type=MESH)

    @pl.when(has_preceding)
    def _():
        pl.semaphore_signal(barrier, inc=1, device_id=device(image - 1, slab), device_id_type=MESH)

    @pl.when(has_following)
    def _():
        pl.semaphore_signal(barrier, inc=1, device_id=device(image + 1, slab), device_id_type=MESH)

    middle = images // 2
    left_end, right_end = image == middle - 1, image == middle
    is_end = jnp.logical_or(left_end, right_end)
    left_relay, right_relay = image < middle - 1, image > middle
    is_relay = jnp.logical_or(left_relay, right_relay)

    @pl.when(is_end)
    def _():
        for n in range(RELAYS):
            for target in (n, middle + n + 1):
                pl.semaphore_signal(
                    barrier, inc=1, device_id=device(target, slab), device_id_type=MESH
                )

    @pl.when(is_relay)
    def _():
        for target in (middle - 1, middle):
            pl.semaphore_signal(
                barrier, inc=1, device_id=device(target, slab), device_id_type=MESH
            )

    loads = [
        pltpu.make_async_copy(
            moment_in.at[0, c], moment.at[c, pl.ds(1, PLANES)], load_sem.at[c]
        )
        for c in range(3)
    ]
    tensor_load = pltpu.make_async_copy(tensor_in, tensor, load_sem.at[3])
    labels_load = pltpu.make_async_copy(labels_in, labels, load_sem.at[4])
    early = [
        pltpu.make_async_copy(source, target, load_sem.at[5 + n])
        for n, (source, target) in enumerate(
            ((z_there_in, z_there), (y_there_in, y_there), (there_in, there))
        )
    ]
    late = [
        pltpu.make_async_copy(source, target, load_sem.at[8 + n])
        for n, (source, target) in enumerate(
            (
                (x_there_in, x_there),
                (x_back_in, x_back),
                (y_back_in, y_back),
                (z_back_in, z_back),
                (back_in, back),
                (anisotropy_in, anisotropy),
                (stiffness_in, stiffness),
            )
        )
    ]
    for load in loads[:1] + early + loads[1:] + [tensor_load] + late + [labels_load]:
        load.start()

    @pl.when(jnp.logical_not(has_preceding))
    def _():
        preceding[...] = jnp.zeros_like(preceding)

    @pl.when(jnp.logical_not(has_following))
    def _():
        following[...] = jnp.zeros_like(following)

    def send_there(c, part):
        @pl.loop(0, SLABS)
        def _(step):
            target = lax.rem(slab + step, SLABS)
            pltpu.make_async_remote_copy(
                src_ref=sending.at[c, pl.ds(part * BLOCK + target * ROWS, ROWS)],
                dst_ref=spectrum.at[c, part, slab],
                send_sem=there_sent.at[c, part],
                recv_sem=there_got.at[c, part],
                device_id=device(other, target),
                device_id_type=MESH,
            ).start()

    def send_back(c, part):
        @pl.loop(0, SLABS)
        def _(step):
            target = lax.rem(slab + step, SLABS)
            pltpu.make_async_remote_copy(
                src_ref=answer.at[c, part, target],
                dst_ref=arrived.at[c, pl.ds(part * BLOCK + slab * ROWS, ROWS)],
                send_sem=back_sent.at[c, part],
                recv_sem=back_got.at[c, part],
                device_id=device(other, target),
                device_id_type=MESH,
            ).start()

    def whole_there(c, part):
        return pltpu.make_async_copy(
            sending.at[c, pl.ds(part * BLOCK, BLOCK)],
            sending.at[c, pl.ds(part * BLOCK, BLOCK)],
            there_sent.at[c, part],
        )

    def whole_spectrum(c, part):
        return pltpu.make_async_copy(
            spectrum.at[c, part], spectrum.at[c, part], there_got.at[c, part]
        )

    def whole_back(c, part):
        return pltpu.make_async_copy(
            answer.at[c, part], answer.at[c, part], back_sent.at[c, part]
        )

    def whole_arrived(c, part):
        return pltpu.make_async_copy(
            arrived.at[c, pl.ds(part * BLOCK, BLOCK)],
            arrived.at[c, pl.ds(part * BLOCK, BLOCK)],
            back_got.at[c, part],
        )

    def remote(source, target, sent, got, of_image, of_slab):
        return pltpu.make_async_remote_copy(
            src_ref=source,
            dst_ref=target,
            send_sem=sent,
            recv_sem=got,
            device_id=device(of_image, of_slab),
            device_id_type=MESH,
        )

    high, low = slab // COLUMN, lax.rem(slab, COLUMN)
    next_high, last_high = lax.rem(high + 1, DEPTH), lax.rem(high + DEPTH - 1, DEPTH)
    at_top, at_bottom = low == COLUMN - 1, low == 0
    strip = G // COLUMN

    def strip_of(plane, n):
        return moment.at[:, plane, pl.ds(n * strip, strip)]

    up_whole = remote(
        moment.at[:, PLANES], moment.at[:, 0], halo_sent.at[0], halo_got.at[0], image, next_slab
    )
    down_whole = remote(
        moment.at[:, 1], moment.at[:, PLANES + 1], halo_sent.at[1], halo_got.at[1], image, last_slab
    )
    up_relay = remote(
        relay_halo.at[0],
        moment.at[:, 0, pl.ds(low * strip, strip)],
        relay_sent.at[1],
        halo_got.at[0],
        image,
        next_high * COLUMN,
    )
    down_relay = remote(
        relay_halo.at[1],
        moment.at[:, PLANES + 1, pl.ds(low * strip, strip)],
        relay_sent.at[2],
        halo_got.at[1],
        image,
        last_high * COLUMN + COLUMN - 1,
    )
    own = moment.at[:, pl.ds(1, PLANES)]
    to_following = remote(
        own, preceding, image_sent.at[0], image_got.at[0], lax.rem(image + 1, images), slab
    )
    to_preceding = remote(
        own, following, image_sent.at[1], image_got.at[1], lax.rem(image + images - 1, images), slab
    )
    share = PLANES // (RELAYS + 1)
    turn = lax.rem(image, middle)
    right_forward = remote(
        relay,
        preceding.at[:, pl.ds(turn * share, share)],
        relay_sent.at[0],
        image_got.at[0],
        middle,
        slab,
    )
    left_forward = remote(
        relay,
        following.at[:, pl.ds(turn * share, share)],
        relay_sent.at[0],
        image_got.at[1],
        middle - 1,
        slab,
    )

    def share_of(n):
        return moment.at[:, pl.ds(1 + n * share, share)]

    def send_near():
        @pl.when(left_end)
        def _():
            for n in range(RELAYS):
                remote(
                    share_of(n), relay, image_sent.at[0], relay_got.at[0], n, slab
                ).start()
            remote(
                share_of(RELAYS),
                preceding.at[:, pl.ds(RELAYS * share, share)],
                image_sent.at[0],
                image_got.at[0],
                middle,
                slab,
            ).start()

        @pl.when(right_end)
        def _():
            for n in range(1, RELAYS + 1):
                remote(
                    share_of(n), relay, image_sent.at[1], relay_got.at[0], middle + n, slab
                ).start()
            remote(
                share_of(0),
                following.at[:, pl.ds(0, share)],
                image_sent.at[1],
                image_got.at[1],
                middle - 1,
                slab,
            ).start()

        @pl.when(at_top)
        def _():
            for n in range(COLUMN - 1):
                remote(
                    strip_of(PLANES, n),
                    relay_halo.at[0],
                    halo_sent.at[0],
                    relay_got.at[1],
                    image,
                    high * COLUMN + n,
                ).start()
            remote(
                strip_of(PLANES, COLUMN - 1),
                strip_of(0, COLUMN - 1),
                halo_sent.at[0],
                halo_got.at[0],
                image,
                next_high * COLUMN,
            ).start()

        @pl.when(at_bottom)
        def _():
            for n in range(1, COLUMN):
                remote(
                    strip_of(1, n),
                    relay_halo.at[1],
                    halo_sent.at[1],
                    relay_got.at[2],
                    image,
                    high * COLUMN + n,
                ).start()
            remote(
                strip_of(1, 0),
                strip_of(PLANES + 1, 0),
                halo_sent.at[1],
                halo_got.at[1],
                image,
                last_high * COLUMN + COLUMN - 1,
            ).start()

        @pl.when(jnp.logical_not(at_top))
        def _():
            up_whole.start()

        @pl.when(jnp.logical_not(at_bottom))
        def _():
            down_whole.start()

        @pl.when(jnp.logical_and(has_following, jnp.logical_not(left_end)))
        def _():
            to_following.start()

        @pl.when(jnp.logical_and(has_preceding, jnp.logical_not(right_end)))
        def _():
            to_preceding.start()

    def forward_strips():
        @pl.when(jnp.logical_not(at_top))
        def _():
            pltpu.make_async_copy(relay_halo.at[0], relay_halo.at[0], relay_got.at[1]).wait()
            up_relay.start()

        @pl.when(jnp.logical_not(at_bottom))
        def _():
            pltpu.make_async_copy(relay_halo.at[1], relay_halo.at[1], relay_got.at[2]).wait()
            down_relay.start()

    def forward_image():
        @pl.when(left_relay)
        def _():
            pltpu.make_async_copy(relay, relay, relay_got.at[0]).wait()
            right_forward.start()

        @pl.when(right_relay)
        def _():
            pltpu.make_async_copy(relay, relay, relay_got.at[0]).wait()
            left_forward.start()

    for c in range(3):
        if c == 0:
            for load in [loads[0]] + early:
                load.wait()

        @pl.loop(0, PLANES // 2)
        def _(step):
            cells = moment[c, pl.ds(1 + 2 * step, 2)].reshape(2 * G, G)
            lines = by_right(cells, z_there)
            both = by_left(y_there, jnp.concatenate([lines[:G], lines[G:]], axis=1))
            for j in range(2):
                cosine, sine = both[:G, j * G : (j + 1) * G], both[G:, j * G : (j + 1) * G]
                values = there[0] * cosine + there[2] * sine
                values = values + turned(there[1] * cosine + there[3] * sine)
                sending[c, pl.ds(2 * step + j, G, stride=8), :] = values

        if c == 0:
            signals = 2 * SLABS - 1 + has_preceding.astype(jnp.int32)
            signals = signals + has_following.astype(jnp.int32) + 2 * is_relay.astype(jnp.int32)
            pl.semaphore_wait(barrier, signals + 2 * RELAYS * is_end.astype(jnp.int32))
        send_there(c, 0)
        if c == 0:
            for load in loads[1:]:
                load.wait()
            send_near()

    for part in range(1, PARTS):
        for c in range(3):
            send_there(c, part)

    forward_strips()

    tensor_load.wait()
    for load in late:
        load.wait()
    lane = lax.broadcasted_iota(jnp.int32, (G, G), 1)

    @pl.loop(0, PLANES)
    def _(row):
        wave = slab * PLANES + row
        first = jnp.logical_and(lane == 0, wave <= HALF)
        middle = jnp.logical_and(lane == HALF, jnp.logical_or(wave == 0, wave >= HALF))
        plain = jnp.logical_and(lane > 0, lane < HALF)
        keep = jnp.logical_or(jnp.logical_or(first, middle), plain)
        for n in range(6):
            values = tensor[n, pl.ds(row, G, stride=8), :]
            packed[n, row] = jnp.where(keep, values, turned(values)) * (-1.0 / G**3)

    real_column = jnp.logical_and(lane % HALF == 0, lax.rem(slab, SLABS // 2) == 0)
    sign = jnp.where(lane < HALF, 1.0, -1.0)

    def multiply(part):
        for c in range(3):
            whole_spectrum(c, part).wait()

        def row_of(row, first):
            def partner(values, factor):
                result = sign * turned(values)
                if first:
                    result = jnp.where(real_column, factor * values, result)
                return result

            at = pl.ds(pl.multiple_of(row * 8, 8), 8)
            lines = [spectrum[c, part, :, at, :].reshape(G, G) for c in range(3)]
            stack = jnp.concatenate(
                [jnp.concatenate([v, partner(v, 1.0)], axis=0) for v in lines], axis=1
            )
            waves = by_left(beside(x_there), stack)
            waves = [waves[:, b * G : (b + 1) * G] for b in range(3)]
            at_row = part * (PLANES // PARTS) + row
            products = []
            for n in TENSOR_ROWS:
                value = packed[n[0], at_row] * waves[0]
                value = value + packed[n[1], at_row] * waves[1]
                products.append(value + packed[n[2], at_row] * waves[2])
            stack = jnp.concatenate(
                [jnp.concatenate([v, partner(v, -1.0)], axis=0) for v in products], axis=1
            )
            result = by_left(beside(x_back), stack)
            for c in range(3):
                answer[c, part, :, at, :] = result[:, c * G : (c + 1) * G].reshape(SLABS, 8, G)

        first = part == 0
        if first:
            row_of(0, True)

        @pl.loop(1 if first else 0, PLANES // PARTS)
        def _(row):
            row_of(row, False)

        for c in range(3):
            send_back(c, part)

    for part in range(PARTS):
        multiply(part)
        if part == 0:
            forward_image()

    labels_load.wait()
    up_whole.wait_recv()
    down_whole.wait_recv()

    @pl.loop(0, PLANES)
    def _(plane):
        region = labels[plane]
        stiff_cell = jnp.zeros((G, G), F32)
        anis_cell = jnp.zeros((G, G), F32)
        for n in range(8):
            stiff_cell = jnp.where(region == n, stiffness[n], stiff_cell)
            anis_cell = jnp.where(region == n, anisotropy[n], anis_cell)
        for c in range(3):
            here = moment[c, plane + 1]
            around = moment[c, plane] + moment[c, plane + 2] - 6.0 * here
            around = around + pltpu.roll(here, 1, 0) + pltpu.roll(here, G - 1, 0)
            around = around + pltpu.roll(here, 1, 1) + pltpu.roll(here, G - 1, 1)
            value = stiff_cell * around
            if c == 2:
                value = value + 2.0 * anis_cell * here
            field[c, plane] = value

    @pl.when(has_preceding)
    def _():
        to_following.wait_recv()

    @pl.when(has_following)
    def _():
        to_preceding.wait_recv()

    def tangent_step(plane, carry):
        here = [moment[c, plane + 1] for c in range(3)]
        before = [preceding[c, plane] for c in range(3)]
        after = [following[c, plane] for c in range(3)]
        change = [after[c] - before[c] for c in range(3)]
        along = change[0] * here[0] + change[1] * here[1] + change[2] * here[2]
        change = [change[c] - along * here[c] for c in range(3)]
        for c in range(3):
            tangent[c, plane] = change[c]
        size = change[0] * change[0] + change[1] * change[1] + change[2] * change[2]
        return (
            carry[0] + tile_sum(size),
            carry[1] + tile_sum(squared_angle(here, after)),
            carry[2] + tile_sum(squared_angle(before, here)),
        )

    zero = jnp.zeros((8, G), F32)
    totals = lax.fori_loop(0, PLANES, tangent_step, (zero, zero, zero))

    def spread(source, targets, n):
        @pl.loop(1, SLABS)
        def _(step):
            remote(
                source,
                targets.at[step - 1],
                sums_out.at[n],
                sums_got.at[n],
                image,
                lax.rem(slab + step, SLABS),
            ).start()

    def collect(source, targets, n):
        pltpu.make_async_copy(targets, targets, sums_got.at[n]).wait()
        return source[...] + jnp.sum(targets[...], axis=0)

    row = lax.broadcasted_iota(jnp.int32, (8, G), 0)
    rows = [jnp.broadcast_to(row_sum(value), (8, G)) for value in totals]
    sums_sent[...] = jnp.where(row == 0, rows[0], jnp.where(row == 1, rows[1], rows[2]))
    spread(sums_sent, sums, 0)

    slope = jnp.zeros((1, G), F32)
    rows_here = G // PARTS
    for part, c in [(part, c) for part in range(PARTS) for c in range(3)]:
        whole_arrived(c, part).wait()
        waves = pl.ds(part * rows_here, rows_here)

        def back_step(step, carry):
            stack = []
            for j in range(2):
                values = arrived[c, pl.ds(part * BLOCK + 2 * step + j, rows_here, stride=8), :]
                first = back[0, waves] * values + turned(back[1, waves] * values)
                second = back[2, waves] * values + turned(back[3, waves] * values)
                stack.append(jnp.concatenate([first, second], axis=0))
            table = [y_back[n, pl.ds(part * G, G)] for n in range(2)]
            lines = by_left(table, jnp.concatenate(stack, axis=1))
            cells = by_right(jnp.concatenate([lines[:, :G], lines[:, G:]], axis=0), z_back)
            at = pl.ds(2 * step, 2)
            whole = field[c, at].reshape(2 * G, G) + cells
            field[c, at] = whole.reshape(2, G, G)
            if part < PARTS - 1:
                return carry
            return carry - row_sum(whole * tangent[c, at].reshape(2 * G, G))

        slope = lax.fori_loop(0, PLANES // 2, back_step, slope)

    slope_sent[...] = slope

    spread(slope_sent, slopes, 1)

    def normal_step(plane, carry):
        here = [moment[c, plane + 1] for c in range(3)]
        gradient = [-field[c, plane] for c in range(3)]
        along = gradient[0] * here[0] + gradient[1] * here[1] + gradient[2] * here[2]
        for c in range(3):
            field[c, plane] = gradient[c] - along * here[c]
        return carry

    lax.fori_loop(0, PLANES, normal_step, 0)
    cells = float(G**3)
    first_sums = collect(sums_sent, sums, 0)
    parts = [whole_sum(jnp.where(row == n, first_sums, 0.0)) for n in range(3)]
    factor = jnp.sqrt(cells / (parts[0] + EPSILON))
    spring = SPRING * (jnp.sqrt(parts[1] / cells) - jnp.sqrt(parts[2] / cells))
    per_slope, constant = factor * factor / cells, spring * factor
    strength = whole_sum(collect(slope_sent, slopes, 1)) * per_slope + constant
    strength_out[...] = jnp.broadcast_to(strength, (1, G))

    for part in range(PARTS):
        for c in range(3):
            whole_there(c, part).wait()
            whole_back(c, part).wait()

    up_whole.wait_send()
    down_whole.wait_send()

    @pl.when(jnp.logical_not(at_top))
    def _():
        up_relay.wait_send()

    @pl.when(jnp.logical_not(at_bottom))
    def _():
        down_relay.wait_send()

    @pl.when(left_relay)
    def _():
        right_forward.wait_send()

    @pl.when(right_relay)
    def _():
        left_forward.wait_send()

    @pl.when(has_following)
    def _():
        to_following.wait_send()

    @pl.when(has_preceding)
    def _():
        to_preceding.wait_send()

    pltpu.make_async_copy(sums, sums, sums_out.at[0]).wait()
    pltpu.make_async_copy(slopes, slopes, sums_out.at[1]).wait()


def step_kernel(
    moment, normal, tangent, strength, path_out, force_out, path, force, store_sem
):
    image = lax.axis_index("image")
    inside = jnp.logical_and(image > 0, image < lax.axis_size("image") - 1)
    movable = jnp.where(inside, 1.0, 0.0)
    chunk = PLANES // STEPS
    stores = []
    factor = strength[...]

    def plane_step(plane, carry):
        stepped = []
        for c in range(3):
            value = movable * (factor * tangent[c, plane] - normal[c, plane])
            force[c, plane] = value
            stepped.append(moment[0, c, plane] + STEP_SIZE * value)
        size = stepped[0] * stepped[0] + stepped[1] * stepped[1] + stepped[2] * stepped[2]
        scale = lax.rsqrt(size)
        for c in range(3):
            path[c, plane] = stepped[c] * scale
        return carry

    for n in range(STEPS):
        lax.fori_loop(n * chunk, (n + 1) * chunk, plane_step, 0)
        at = pl.ds(n * chunk, chunk)
        stores.append(
            pltpu.make_async_copy(path.at[:, at], path_out.at[0, :, at], store_sem.at[0, n])
        )
        stores.append(
            pltpu.make_async_copy(force.at[:, at], force_out.at[0, :, at], store_sem.at[1, n])
        )
        stores[-2].start()
        stores[-1].start()
    for store in stores:
        store.wait()


def local(magnetization, region_labels, demag_kernel, anisotropy, stiffness):
    block = (3, PLANES, G, G)
    shape = jax.ShapeDtypeStruct((1,) + block, F32)
    hbm_spec = pl.BlockSpec(memory_space=pltpu.HBM)
    vmem_spec = pl.BlockSpec(memory_space=pltpu.VMEM)

    def in_hbm(array):
        return pltpu.with_memory_space_constraint(array, pltpu.HBM)

    constants = [jnp.asarray(table) for table in tables()]
    dma = pltpu.SemaphoreType.DMA
    normal, tangent, strength = pl.pallas_call(
        kernel,
        out_shape=(
            pltpu.VMEM(block, F32),
            pltpu.VMEM(block, F32),
            pltpu.VMEM((1, G), F32),
        ),
        in_specs=[hbm_spec] * (5 + len(constants)),
        out_specs=(vmem_spec, vmem_spec, vmem_spec),
        scratch_shapes=[
            pltpu.SMEM((8,), F32),
            pltpu.SMEM((8,), F32),
            *(pltpu.VMEM(table.shape, table.dtype) for table in constants),
            pltpu.VMEM((3, PLANES + 2, G, G), F32),
            pltpu.VMEM((PLANES, G, G), jnp.int32),
            pltpu.VMEM((6, G * PLANES, G), F32),
            pltpu.VMEM((6, PLANES, G, G), F32),
            pltpu.VMEM((3, PARTS * BLOCK, G), F32),
            pltpu.VMEM((3, PARTS, SLABS, ROWS, G), F32),
            pltpu.VMEM((3, PARTS, SLABS, ROWS, G), F32),
            pltpu.VMEM((3, PARTS * BLOCK, G), F32),
            pltpu.VMEM(block, F32),
            pltpu.VMEM(block, F32),
            pltpu.VMEM((3, PLANES // (RELAYS + 1), G, G), F32),
            pltpu.VMEM((2, 3, G // COLUMN, G), F32),
            pltpu.VMEM((8, G), F32),
            pltpu.VMEM((SLABS - 1, 8, G), F32),
            pltpu.VMEM((1, G), F32),
            pltpu.VMEM((SLABS - 1, 1, G), F32),
            dma((15,)),
            dma((3, PARTS)),
            dma((3, PARTS)),
            dma((3, PARTS)),
            dma((3, PARTS)),
            dma((2,)),
            dma((2,)),
            dma((2,)),
            dma((2,)),
            dma((3,)),
            dma((3,)),
            dma((2,)),
            dma((2,)),
        ],
        compiler_params=pltpu.CompilerParams(
            collective_id=0, has_side_effects=True, vmem_limit_bytes=40 * 2**20
        ),
    )(
        in_hbm(magnetization),
        in_hbm(region_labels),
        in_hbm(demag_kernel.reshape(6, G * PLANES, G)),
        in_hbm(anisotropy),
        in_hbm(stiffness),
        *(in_hbm(constant) for constant in constants),
    )
    return pl.pallas_call(
        step_kernel,
        out_shape=(shape, shape),
        in_specs=[vmem_spec] * 4,
        out_specs=(hbm_spec, hbm_spec),
        scratch_shapes=[pltpu.VMEM(block, F32)] * 2 + [dma((2, STEPS))],
        compiler_params=pltpu.CompilerParams(vmem_limit_bytes=STEP_LIMIT * 2**20),
    )(magnetization, normal, tangent, strength)


def solution(mesh):
    in_specs = (
        P("image", None, "space", None, None),
        P("space", None, None),
        P(None, None, "space", None),
        P(),
        P(),
    )
    out_specs = (P("image", None, "space", None, None), P("image", None, "space", None, None))
    return jax.shard_map(local, mesh=mesh, in_specs=in_specs, out_specs=out_specs, check_vma=False)
```
